256 devices in a mesh: grp: 8 (over y, core), dev: 32 (over x, z).
Axes of the slice: x: 4, y: 4, z: 8, core: 2. Of those that a mesh axis runs over, the one named last changes fastest.
Arguments:
- strengths: bfloat16 [131072, 256], P(('grp', 'dev')), may hold values from 0.099609375 to 1
- source_counts: int32 [131072], P(('grp', 'dev')), may hold values from 1 to 256
- source_map: bfloat16 [256, 98], replicated, may hold values from -0.375 to 0.375
- merge_ops: bfloat16 [8, 98, 98], replicated, may hold values from -0.21875 to 0.21875
- translate_ops: bfloat16 [189, 98, 98], replicated, may hold values from -0.046875 to 0.046875
- spread_ops: bfloat16 [8, 98, 98], replicated, may hold values from -0.625 to 0.625
- leaf_lists: int32 [189, 131072], P(None, ('grp', 'dev')), may hold values from -1 to 1023, as said below
- parent_lists: int32 [189, 16384], P(None, ('grp', 'dev')), may hold values from -1 to 127, as said below
- grand_lists: int32 [189, 2048], P(None, ('grp', 'dev')), may hold values from -1 to 15, as said below
- top_lists: int32 [189, 256], P(None, ('grp', 'dev')), may hold values from -1 to 255, as said below
Outputs:
- leaf_local: float32 [98, 131072], P(None, ('grp', 'dev'))
The draws below stay inside these ranges and needn't reach their ends.
Inputs may be any that keep to these rules, and one draw needn't show every extreme that they name: `leaf_lists`: each entry is -1 or names an existing leaf box; both ends of the range are reached in every draw. `parent_lists`: each entry is -1 or names an existing box of that level; both ends are reached. `grand_lists`: each entry is -1 or names an existing box of that level; both ends are reached. `top_lists`: each entry is -1 or any box of that level.
All inputs are finite; a program needn't handle non-finite values.
Results may differ from the reference program's by a relative error of at most 0.0055.
Values may be sent and summed in bfloat16 or wider, within the bound.
A program may use at most 128 MiB of HBM per device.

```python
import math
import jax
import jax.numpy as jnp
from jax import lax

P_SIZE = 98
NCLASS = 189
SLOTS = 256
LEAF_DEV = 512
PARENT_DEV = 64
GRAND_DEV = 8
TOP_DEV = 1
NLEAF = 131072
NPARENT = 16384
NGRAND = 2048
NTOP = 256


def level_table(key, kcount, per_dev, total, reach):
    box_ids = jnp.arange(total, dtype=jnp.int32)
    first_box = box_ids // per_dev * per_dev
    low_end = jnp.maximum(first_box - reach, 0)
    high_end = jnp.minimum(first_box + per_dev + reach, total)
    key_pick, key_live = jax.random.split(key)
    raw_draw = jax.random.randint(key_pick, (kcount, total), 0, 1 << 30, dtype=jnp.int32)
    chosen = low_end[None, :] + raw_draw % (high_end - low_end)[None, :]
    is_live = jax.random.randint(key_live, (kcount, total), 0, 5, dtype=jnp.int32) < 3
    entries = jnp.where(is_live, chosen, -1)
    entries = entries.at[0].set(jnp.where(box_ids == first_box, low_end, entries[0]))
    entries = entries.at[1].set(jnp.where(box_ids == first_box + per_dev - 1, high_end - 1, entries[1]))
    entries = entries.at[2, 0].set(-1)
    return entries.astype(jnp.int32)


def relative_table(key, kcount, per_dev, total):
    entries = level_table(key, kcount, per_dev, total, per_dev // 2)
    box_ids = jnp.arange(total, dtype=jnp.int32)
    anchor = box_ids // per_dev * per_dev - per_dev // 2
    return jnp.where(entries >= 0, entries - anchor[None, :], -1).astype(jnp.int32)


def draw_leaf_lists(key, part):
    key = jax.random.fold_in(key, 11)
    return relative_table(key, NCLASS, LEAF_DEV, NLEAF)


def draw_parent_lists(key, part):
    key = jax.random.fold_in(key, 12)
    return relative_table(key, NCLASS, PARENT_DEV, NPARENT)


def draw_grand_lists(key, part):
    key = jax.random.fold_in(key, 13)
    return relative_table(key, NCLASS, GRAND_DEV, NGRAND)


def draw_top_lists(key, part):
    key = jax.random.fold_in(key, 14)
    return level_table(key, NCLASS, TOP_DEV, NTOP, NTOP)


def plant(values, key, smallest, top_value):
    index_at = [jax.random.randint(jax.random.fold_in(key, axis), (), 0, length) for axis, length in enumerate(values.shape)]
    main_axis = values.shape.index(max(values.shape))
    neighbour = index_at[:main_axis] + [(index_at[main_axis] + 1) % values.shape[main_axis]] + index_at[main_axis + 1:]
    return values.at[tuple(index_at)].set(smallest).at[tuple(neighbour)].set(top_value)


def block_levels(own_key, dims, pieces, least, top_value):
    factor_of = 1.0
    for position, shards_of in pieces:
        draws = jax.random.uniform(jax.random.fold_in(jax.random.fold_in(own_key, 6), position), (shards_of,), jnp.float32, least / len(pieces), top_value / len(pieces))
        factor_of = factor_of * jnp.repeat(jnp.exp(draws), dims[position] // shards_of).reshape((-1,) + (1,) * (len(dims) - 1 - position))
    return factor_of


def centred(rng, dims, width, most, held_as=jnp.bfloat16):
    values = jax.random.normal(rng, dims, jnp.float32) * width
    return jnp.minimum(jnp.maximum(values, -most), most).astype(held_as)


def setup_inputs(seed: int = 0) -> dict:
    streams_of = jax.random.split(jax.random.key(seed), 11)
    strengths = jnp.clip(jnp.exp(math.log(1.0) - 2.306499 * jax.random.uniform(streams_of[0], (NLEAF, SLOTS), jnp.float32) ** block_levels(streams_of[0], (NLEAF, SLOTS), ((0, 256),), -0.2, 0.2)), 0.099609375, 1.0).astype(jnp.bfloat16)
    source_counts = plant(jax.random.randint(streams_of[1], (NLEAF,), 1, SLOTS + 1), jax.random.fold_in(streams_of[1], 1), 1, SLOTS).astype(jnp.int32)
    source_map = centred(streams_of[2], (SLOTS, P_SIZE), SLOTS ** -0.5, 0.375)
    merge_ops = centred(streams_of[3], (8, P_SIZE, P_SIZE), (8 * P_SIZE) ** -0.5, 0.21875)
    translate_ops = centred(streams_of[4], (NCLASS, P_SIZE, P_SIZE), (NCLASS * P_SIZE) ** -0.5, 0.046875)
    spread_ops = centred(streams_of[5], (8, P_SIZE, P_SIZE), P_SIZE ** -0.5, 0.625)
    leaf_lists = draw_leaf_lists(jax.random.fold_in(streams_of[10], 71), 0)
    parent_lists = draw_parent_lists(jax.random.fold_in(streams_of[10], 71), 0)
    grand_lists = draw_grand_lists(jax.random.fold_in(streams_of[10], 71), 0)
    top_lists = draw_top_lists(jax.random.fold_in(streams_of[10], 71), 0)
    return dict(strengths=strengths, source_counts=source_counts, source_map=source_map, merge_ops=merge_ops, translate_ops=translate_ops, spread_ops=spread_ops, leaf_lists=leaf_lists, parent_lists=parent_lists, grand_lists=grand_lists, top_lists=top_lists)


def sources_up(strengths, source_counts, source_map):
    slot_ids = jnp.arange(strengths.shape[1], dtype=jnp.int32)
    is_live = slot_ids[None, :] < source_counts[:, None]
    masked = jnp.where(is_live, strengths, jnp.zeros_like(strengths))
    return lax.dot_general(source_map, masked, (((0,), (1,)), ((), ())), preferred_element_type=jnp.float32).astype(jnp.bfloat16)


def merge_children(child_m, merge_ops):
    grouped = child_m.reshape(child_m.shape[0], child_m.shape[1] // 8, 8).astype(jnp.float32)
    return jnp.einsum("cqp,pjc->qj", merge_ops.astype(jnp.float32), grouped).astype(jnp.bfloat16)


def spread_children(parent_local, spread_ops):
    rounded = lax.optimization_barrier(parent_local.astype(jnp.bfloat16)).astype(jnp.float32)
    children = jnp.einsum("cqp,pj->qjc", spread_ops.astype(jnp.float32), rounded)
    return children.reshape(children.shape[0], -1)


def translate_block(window, table_rows, operators):
    kcount = table_rows.shape[0]
    block_size = -(-kcount // 4)
    summed = jnp.zeros((window.shape[0], table_rows.shape[1]), jnp.float32)
    for first_class in range(0, kcount, block_size):
        class_rows = table_rows[first_class:first_class + block_size]
        is_valid = class_rows >= 0
        picked = jnp.take(window, jnp.clip(class_rows, 0, window.shape[1] - 1).astype(jnp.int32), axis=1)
        picked = jnp.where(is_valid[None], picked, jnp.zeros_like(picked))
        summed = summed + jnp.einsum("kqp,pkn->qn", operators[first_class:first_class + block_size].astype(jnp.float32), picked.astype(jnp.float32))
    return summed


def level_far(multipoles, lists, operators, per_dev, factor, relative):
    block_count = lists.shape[1] // per_dev
    blocks = lists.reshape(lists.shape[0], block_count, per_dev).transpose(1, 0, 2)
    block_ids = jnp.arange(block_count, dtype=jnp.int32)

    def per_block(item):
        table_rows, block_id = item
        if relative:
            shift_by = (block_id * per_dev - per_dev // 2).astype(jnp.int32)
            table_rows = jnp.where(table_rows >= 0, table_rows + shift_by, -1).astype(jnp.int32)
        return translate_block(multipoles, table_rows, operators)

    result = lax.map(per_block, (blocks, block_ids))
    return factor * result.transpose(1, 0, 2).reshape(multipoles.shape[0], -1)


def reference(strengths, source_counts, source_map, merge_ops, translate_ops, spread_ops, leaf_lists, parent_lists, grand_lists, top_lists):
    leaf_m = sources_up(strengths, source_counts, source_map)
    parent_m = merge_children(leaf_m, merge_ops)
    grand_m = merge_children(parent_m, merge_ops)
    top_m = merge_children(grand_m, merge_ops)
    top_local = level_far(top_m, top_lists, translate_ops, TOP_DEV, 0.125, False)
    grand_local = level_far(grand_m, grand_lists, translate_ops, GRAND_DEV, 0.25, True) + spread_children(top_local, spread_ops)
    parent_local = level_far(parent_m, parent_lists, translate_ops, PARENT_DEV, 0.5, True) + spread_children(grand_local, spread_ops)
    return level_far(leaf_m, leaf_lists, translate_ops, LEAF_DEV, 1.0, True) + spread_children(parent_local, spread_ops)
```

```python
import jax
import jax.numpy as jnp
from jax import lax
from jax.experimental import pallas as pl
from jax.experimental.pallas import tpu as pltpu
from jax.sharding import PartitionSpec as P

BF = jnp.bfloat16
F32 = jnp.float32
ROWS = 104
MESH = pl.DeviceIdType.MESH
NT = (((1,), (1,)), ((), ()))


def up_kernel(
    grps, devs, strengths, counts, smap, mg, leaf_out, mid_out, top_out,
    m_ref, leaf_t, par_t, gra_t, mine, got, midm, midg, msg, buf_a, msg_b, buf_b,
    send_l, recv_l, send_m, recv_m, send_a, recv_a, send_b, recv_b,
):
    g = lax.axis_index("grp")
    d = lax.axis_index("dev")
    total = grps * devs
    me = g * devs + d
    above = lax.rem(me + 1, total)
    below = lax.rem(me + total - 1, total)

    def at(pos):
        return (pos // devs, lax.rem(pos, devs))

    barrier = pltpu.get_barrier_semaphore()

    def greet(pos):
        pl.semaphore_signal(barrier, inc=1, device_id=pos, device_id_type=MESH)

    greet(at(above))
    greet(at(below))
    lax.fori_loop(1, grps, lambda i, c: (greet((lax.rem(g + i, grps), d)), c)[1], 0)
    lax.fori_loop(1, devs, lambda i, c: (greet((g, lax.rem(d + i, devs))), c)[1], 0)

    cnt = jnp.concatenate(
        [jnp.broadcast_to(counts[:, 128 * i : 128 * i + 128], (128, 128)).T for i in range(4)], axis=0
    ).astype(jnp.int16)
    slot = lax.broadcasted_iota(jnp.int16, (512, 128), 1)
    zero = jnp.zeros((512, 128), BF)
    live = jnp.concatenate(
        [
            jnp.where(slot < cnt, strengths[:, 0:128], zero),
            jnp.where(slot + jnp.int16(128) < cnt, strengths[:, 128:256], zero),
        ],
        axis=1,
    )
    leaf_t[...] = jnp.zeros_like(leaf_t)
    par_t[...] = jnp.zeros_like(par_t)
    gra_t[...] = jnp.zeros_like(gra_t)
    m_ref[...] = jnp.zeros_like(m_ref)
    lt = lax.dot_general(live, smap[...], NT, preferred_element_type=F32)
    leaf_t[:, 0:98] = lt.astype(BF).astype(F32)
    for half in range(2):
        mine[half] = jnp.concatenate(
            [leaf_t[256 * half + 128 * i : 256 * half + 128 * i + 128, :].T[0:112] for i in range(2)], axis=1
        ).astype(BF)

    def copy(src, dst, ss, rs, pos):
        return pltpu.make_async_remote_copy(
            src_ref=src, dst_ref=dst, send_sem=ss, recv_sem=rs, device_id=pos, device_id_type=MESH
        )

    pl.semaphore_wait(barrier, 2 + grps - 1 + devs - 1)
    leaf_up = copy(mine.at[1], got.at[0], send_l.at[0], recv_l.at[0], at(above))
    leaf_dn = copy(mine.at[0], got.at[1], send_l.at[1], recv_l.at[1], at(below))
    leaf_up.start()
    leaf_dn.start()

    for q in range(98):
        m_ref[pl.ds(q, 8, stride=ROWS), 0:98] = mg[q].astype(F32)
    merge = jnp.concatenate([m_ref[ROWS * c : ROWS * c + ROWS, :].astype(BF) for c in range(8)], axis=1)

    def merged(kids):
        x = jnp.concatenate([k.astype(BF) for k in kids], axis=1)
        y = lax.dot_general(x, merge, NT, preferred_element_type=F32)
        return y.astype(BF).astype(F32)

    par_t[:, 0:ROWS] = merged([leaf_t[pl.ds(c, 64, stride=8), :] for c in range(8)])
    gra_t[:, 0:ROWS] = merged([par_t[pl.ds(c, 8, stride=8), :] for c in range(8)])
    msg[...] = jnp.zeros_like(msg)
    msg[:, 0:ROWS] = merged([jnp.broadcast_to(gra_t[c : c + 1, :], (8, 128)) for c in range(8)])

    def send_top(i, c):
        to = lax.rem(g + i, grps)
        copy(msg, buf_a.at[g], send_a.at[i], recv_a.at[g], (to, d)).start()
        return c

    lax.fori_loop(1, grps, send_top, 0)

    both = jnp.concatenate([par_t[...], gra_t[...], jnp.zeros((56, 128), F32)], axis=0)
    midm[...] = both.T[0:112].astype(BF)
    mid_up = copy(midm, midg.at[0], send_m.at[0], recv_m.at[0], at(above))
    mid_dn = copy(midm, midg.at[1], send_m.at[1], recv_m.at[1], at(below))
    mid_up.start()
    mid_dn.start()

    sub = lax.broadcasted_iota(jnp.int32, (8, 128), 0)

    def wait_top(i, c):
        frm = lax.rem(g + i, grps)
        w = copy(msg, buf_a.at[frm], send_a.at[i], recv_a.at[frm], (frm, d))
        w.wait_send()
        w.wait_recv()
        return jnp.where(sub == frm, buf_a[frm], c)

    msg_b[...] = lax.fori_loop(1, grps, wait_top, msg[...])

    def send_block(i, c):
        to = lax.rem(d + i, devs)
        copy(msg_b, buf_b.at[d], send_b.at[i], recv_b.at[d], (g, to)).start()
        return c

    lax.fori_loop(1, devs, send_block, 0)
    leaf_up.wait()
    leaf_dn.wait()
    leaf_out[0] = got[0]
    leaf_out[1] = mine[0]
    leaf_out[2] = mine[1]
    leaf_out[3] = got[1]
    mid_up.wait()
    mid_dn.wait()
    mid_out[0] = midg[0]
    mid_out[1] = midm[...]
    mid_out[2] = midg[1]

    def wait_block(i, c):
        frm = lax.rem(d + i, devs)
        w = copy(msg_b, buf_b.at[frm], send_b.at[i], recv_b.at[frm], (g, frm))
        w.wait_send()
        w.wait_recv()
        top_out[frm] = buf_b[frm]
        return c

    top_out[d] = msg_b[...]
    lax.fori_loop(1, devs, wait_block, 0)


def go_up(mesh, strengths, counts, smap, mg):
    grps, devs = mesh.shape["grp"], mesh.shape["dev"]
    vmem = pl.BlockSpec(memory_space=pltpu.VMEM)
    dma = pltpu.SemaphoreType.DMA
    return pl.pallas_call(
        lambda *refs: up_kernel(grps, devs, *refs),
        out_shape=(
            jax.ShapeDtypeStruct((4, 112, 256), BF),
            jax.ShapeDtypeStruct((3, 112, 128), BF),
            jax.ShapeDtypeStruct((devs, grps, 128), F32),
        ),
        in_specs=[vmem] * 4,
        out_specs=(vmem,) * 3,
        scratch_shapes=[
            pltpu.VMEM((8 * ROWS, 128), F32),
            pltpu.VMEM((512, 128), F32),
            pltpu.VMEM((64, 128), F32),
            pltpu.VMEM((8, 128), F32),
            pltpu.VMEM((2, 112, 256), BF),
            pltpu.VMEM((2, 112, 256), BF),
            pltpu.VMEM((112, 128), BF),
            pltpu.VMEM((2, 112, 128), BF),
            pltpu.VMEM((8, 128), F32),
            pltpu.VMEM((grps, 8, 128), F32),
            pltpu.VMEM((8, 128), F32),
            pltpu.VMEM((devs, 8, 128), F32),
            dma((2,)), dma((2,)), dma((2,)), dma((2,)),
            dma((grps,)), dma((grps,)), dma((devs,)), dma((devs,)),
        ],
        compiler_params=pltpu.CompilerParams(
            collective_id=0, has_side_effects=True, vmem_limit_bytes=24 << 20
        ),
        name="up_and_exchange",
    )(strengths, counts, smap, mg)


def take_lanes(x, index):
    dims = lax.GatherDimensionNumbers(
        offset_dims=(),
        collapsed_slice_dims=(1,),
        start_index_map=(1,),
        operand_batching_dims=(0,),
        start_indices_batching_dims=(0,),
    )
    return lax.gather(
        x, index[..., None], dims, slice_sizes=(1, 1), mode=lax.GatherScatterMode.PROMISE_IN_BOUNDS
    )


def far_kernel(
    leaf_w, mid_w, tops, leaf_lists, par_l, gra_l, top_l, tr, sp, out,
    w4, pwin, gwin, twin, g_ref, a_ref, s_ref, ml_ref, mt_ref, acc_ref,
):
    nclass = leaf_lists.shape[0]
    w4[...] = jnp.concatenate([leaf_w[h].astype(F32)[0:ROWS] for h in range(4)], axis=0).astype(BF)
    at = lax.broadcasted_iota(jnp.int16, (16, 128), 1)
    for v in range(7):
        rows = slice(16 * v, 16 * v + 16)
        low, own, high = mid_w[0, rows, :], mid_w[1, rows, :], mid_w[2, rows, :]
        pwin[rows, :] = jnp.where(
            at < 32,
            take_lanes(low, (at + jnp.int16(32)) & jnp.int16(127)),
            jnp.where(
                at < 96,
                take_lanes(own, (at - jnp.int16(32)) & jnp.int16(127)),
                take_lanes(high, (at - jnp.int16(96)) & jnp.int16(127)),
            ),
        )
        gwin[rows, :] = jnp.where(
            at < 4,
            take_lanes(low, (at + jnp.int16(68)) & jnp.int16(127)),
            jnp.where(
                at < 12,
                take_lanes(own, (at + jnp.int16(60)) & jnp.int16(127)),
                take_lanes(high, (at + jnp.int16(52)) & jnp.int16(127)),
            ),
        )
    for i in range(2):
        twin[:, 128 * i : 128 * i + 128] = tops[128 * i : 128 * i + 128, :].T[0:112].astype(BF)
    g_ref[...] = jnp.zeros_like(g_ref)
    a_ref[...] = jnp.zeros_like(a_ref)
    s_ref[...] = jnp.zeros_like(s_ref)
    acc_ref[...] = jnp.zeros_like(acc_ref)
    ml_ref[...] = jnp.full_like(ml_ref, -1)
    ml_ref[0:64, 0:nclass] = par_l[...]
    ml_ref[64:72, 0:nclass] = gra_l[...]
    t = top_l[...]
    ml_ref[72:73, 0:nclass] = jnp.where(t >= 0, (t & 31) * 8 + (t >> 5), -1)
    mt_ref[0:128, :] = ml_ref[:, 0:128].T
    mt_ref[128:256, :] = ml_ref[:, 128:256].T
    for q in range(98):
        s_ref[pl.ds(q, 8, stride=ROWS), 0:98] = sp[q].astype(F32)

    sub = lax.broadcasted_iota(jnp.int16, (16, 512), 0)
    lane = lax.broadcasted_iota(jnp.int32, (16, 128), 1)

    def leaf_class(row, base):
        lo = jnp.broadcast_to(row & 255, (16, 512)).astype(jnp.int16)
        hi = row >> 8
        onehot = jnp.concatenate(
            [
                jnp.where(lo - jnp.int16(16 * g) == sub, BF(1), BF(0))
                for g in range(16)
            ],
            axis=0,
        )
        r = jnp.dot(w4[...], onehot, preferred_element_type=F32)
        picked = jnp.zeros((ROWS, 512), F32)
        for h in range(4):
            hit = jnp.broadcast_to(hi == h, (ROWS, 512))
            picked = jnp.where(hit, r[h * ROWS : (h + 1) * ROWS], picked)
        g_ref[base : base + ROWS, 0:512] = picked.astype(BF)

    def mid_class(row, base):
        e = jnp.broadcast_to(row, (16, 128))
        lo = (e & 127).astype(jnp.int16)
        is_p = ((lane < 64) & (e >= 0)).astype(jnp.int16) > 0
        is_g = ((lane >= 64) & (lane < 72) & (e >= 0)).astype(jnp.int16) > 0
        is_t0 = ((lane == 72) & (e >= 0) & (e < 128)).astype(jnp.int16) > 0
        is_t1 = ((lane == 72) & (e >= 128)).astype(jnp.int16) > 0
        for v in range(7):
            rows = slice(16 * v, 16 * v + 16)
            x = jnp.zeros((16, 128), BF)
            x = jnp.where(is_p, take_lanes(pwin[rows, :], lo), x)
            x = jnp.where(is_g, take_lanes(gwin[rows, :], lo), x)
            x = jnp.where(is_t0, take_lanes(twin[rows, 0:128], lo), x)
            x = jnp.where(is_t1, take_lanes(twin[rows, 128:256], lo), x)
            g_ref[base + 16 * v : base + 16 * v + 16, 512:640] = x

    def group(k0, n):
        for q in range(98):
            a_ref[pl.ds(q, n, stride=ROWS), 0:98] = tr[q, pl.ds(k0, n), :].astype(F32)
        lists = [leaf_lists[pl.ds(k0 + s, min(8, n - s)), :] for s in range(0, n, 8)]
        mids = [mt_ref[pl.ds(k0 + s, min(8, n - s)), :] for s in range(0, n, 8)]
        for c in range(n):
            leaf_class(lists[c // 8][c % 8 : c % 8 + 1], c * 128)
            mid_class(mids[c // 8][c % 8 : c % 8 + 1], c * 128)
        for s in range(0, n, 8):
            m = min(8, n - s)
            ops = jnp.concatenate(
                [a_ref[(s + c) * ROWS : (s + c + 1) * ROWS, :].astype(BF) for c in range(m)], axis=1
            )
            acc_ref[...] += jnp.dot(
                ops, g_ref[s * 128 : (s + m) * 128, :], preferred_element_type=F32
            )

    full = nclass // 16

    def step(j, carry):
        group(pl.multiple_of(j * 16, 16), 16)
        return carry

    lax.fori_loop(0, full, step, 0)
    group(full * 16, nclass - full * 16)

    spread = s_ref[...].astype(BF)
    lane = lax.broadcasted_iota(jnp.int32, (ROWS, 128), 1)

    def spread_from(x, index):
        picked = take_lanes(x, index).astype(BF)
        z = jnp.dot(
            spread,
            jnp.concatenate([picked, jnp.zeros((128 - ROWS, 128), BF)], axis=0),
            preferred_element_type=F32,
        )
        r = z[0:ROWS]
        for c in range(1, 8):
            r = jnp.where((lane & 7) == c, z[c * ROWS : (c + 1) * ROWS], r)
        return r

    mid = acc_ref[:, 512:640]
    grand = 0.25 * mid + spread_from(0.125 * mid, jnp.full((ROWS, 128), 72, jnp.int32))
    parent = 0.5 * mid + spread_from(grand, 64 + ((lane >> 3) & 7))
    for g in range(4):
        cols = slice(128 * g, 128 * g + 128)
        out[:, cols] = (acc_ref[:, cols] + spread_from(parent, 16 * g + (lane >> 3)))[0:98]


def far_all(leaf_w, mid_w, tops, leaf_lists, par_l, gra_l, top_l, tr, sp):
    p, nclass, leaves = tr.shape[0], tr.shape[1], leaf_lists.shape[1]
    vmem = pl.BlockSpec(memory_space=pltpu.VMEM)
    return pl.pallas_call(
        far_kernel,
        out_shape=jax.ShapeDtypeStruct((p, leaves), F32),
        in_specs=[vmem] * 9,
        out_specs=vmem,
        scratch_shapes=[
            pltpu.VMEM((4 * ROWS, 256), BF),
            pltpu.VMEM((112, 128), BF),
            pltpu.VMEM((112, 128), BF),
            pltpu.VMEM((112, 256), BF),
            pltpu.VMEM((16 * 128, 640), BF),
            pltpu.VMEM((16 * ROWS, 128), F32),
            pltpu.VMEM((8 * ROWS, 128), F32),
            pltpu.VMEM((128, 256), jnp.int32),
            pltpu.VMEM((256, 128), jnp.int32),
            pltpu.VMEM((ROWS, 640), F32),
        ],
        compiler_params=pltpu.CompilerParams(vmem_limit_bytes=40 << 20),
        name="far_field",
    )(leaf_w, mid_w, tops, leaf_lists, par_l, gra_l, top_l, tr, sp)


def solution(mesh):
    def per_device(
        strengths, source_counts, source_map, merge_ops, translate_ops, spread_ops,
        leaf_lists, parent_lists, grand_lists, top_lists,
    ):
        leaf_w, mid_w, tops = go_up(
            mesh, strengths, source_counts.reshape(1, -1), source_map.T, merge_ops.transpose(1, 0, 2)
        )
        return far_all(
            leaf_w, mid_w, tops.reshape(-1, 128), leaf_lists, parent_lists.T, grand_lists.T, top_lists.T,
            translate_ops.transpose(1, 0, 2), spread_ops.transpose(1, 0, 2),
        )

    spread_out = P(("grp", "dev"))
    cols = P(None, ("grp", "dev"))
    return jax.shard_map(
        per_device,
        mesh=mesh,
        in_specs=(P(("grp", "dev"), None), spread_out, P(), P(), P(), P(), cols, cols, cols, cols),
        out_specs=cols,
        check_vma=False,
    )
```

```python
import jax
import jax.numpy as jnp
from jax import lax
from jax.experimental import pallas as pl
from jax.experimental.pallas import tpu as pltpu
from jax.sharding import PartitionSpec as P

BF = jnp.bfloat16
F32 = jnp.float32
ROWS = 104
MESH = pl.DeviceIdType.MESH
NT = (((1,), (1,)), ((), ()))


def take_lanes(x, index):
    dims = lax.GatherDimensionNumbers(
        offset_dims=(),
        collapsed_slice_dims=(1,),
        start_index_map=(1,),
        operand_batching_dims=(0,),
        start_indices_batching_dims=(0,),
    )
    return lax.gather(
        x, index[..., None], dims, slice_sizes=(1, 1), mode=lax.GatherScatterMode.PROMISE_IN_BOUNDS
    )


def kernel(
    grps, devs,
    strengths_h, counts_h, smap_h, mg_h, leaf_lists_h, par_h, gra_h, top_h, tr_h, sp_h, out,
    strengths, counts, smap, mg, leaf_lists, par_l, gra_l, top_l, tr, sp,
    m_ref, leaf_t, par_t, gra_t, mine, got, midm, midg, msg, buf_a, msg_b, buf_b, tops,
    w4, pwin, gwin, g_ref, a_ref, s_ref, ml_ref, mt_ref, acc_ref, tsum_ref,
    load_sem, send_l, recv_l, send_m, recv_m, send_a, recv_a, send_b, recv_b,
):
    g = lax.axis_index("grp")
    d = lax.axis_index("dev")
    total = grps * devs
    me = g * devs + d
    above = lax.rem(me + 1, total)
    below = lax.rem(me + total - 1, total)

    def at(pos):
        return (pos // devs, lax.rem(pos, devs))

    def load(src, dst, k):
        c = pltpu.make_async_copy(src, dst, load_sem.at[k])
        c.start()
        return c

    strengths_in = load(strengths_h, strengths, 0)
    counts_in = load(counts_h, counts, 1)
    smap_in = load(smap_h, smap, 2)
    mg_in = load(mg_h, mg, 3)
    lists_in = [
        load(h, v, 4 + i)
        for i, (h, v) in enumerate(
            ((leaf_lists_h, leaf_lists), (par_h, par_l), (gra_h, gra_l), (top_h, top_l), (sp_h, sp))
        )
    ]
    tr_in = load(tr_h, tr, 9)
    barrier = pltpu.get_barrier_semaphore()

    def greet(pos):
        pl.semaphore_signal(barrier, inc=1, device_id=pos, device_id_type=MESH)

    greet(at(above))
    greet(at(below))
    lax.fori_loop(1, grps, lambda i, c: (greet((lax.rem(g + i, grps), d)), c)[1], 0)
    lax.fori_loop(1, devs, lambda i, c: (greet((g, lax.rem(d + i, devs))), c)[1], 0)

    for r in (leaf_t, par_t, gra_t, m_ref, a_ref, s_ref, acc_ref, tsum_ref):
        r[...] = jnp.zeros_like(r)
    g_ref[...] = jnp.zeros_like(g_ref)
    ml_ref[...] = jnp.full_like(ml_ref, -1)
    for r in (strengths_in, counts_in, smap_in):
        r.wait()
    cnt = jnp.concatenate(
        [jnp.broadcast_to(counts[:, 128 * i : 128 * i + 128], (128, 128)).T for i in range(4)], axis=0
    ).astype(jnp.int16)
    slot = lax.broadcasted_iota(jnp.int16, (512, 128), 1)
    zero = jnp.zeros((512, 128), BF)
    live = jnp.concatenate(
        [
            jnp.where(slot < cnt, strengths[:, 0:128], zero),
            jnp.where(slot + jnp.int16(128) < cnt, strengths[:, 128:256], zero),
        ],
        axis=1,
    )
    lt = lax.dot_general(live, smap[...], NT, preferred_element_type=F32)
    leaf_t[:, 0:98] = lt.astype(BF).astype(F32)
    for half in range(2):
        mine[half] = jnp.concatenate(
            [leaf_t[256 * half + 128 * i : 256 * half + 128 * i + 128, :].T[0:112] for i in range(2)], axis=1
        ).astype(BF)

    def copy(src, dst, ss, rs, pos):
        return pltpu.make_async_remote_copy(
            src_ref=src, dst_ref=dst, send_sem=ss, recv_sem=rs, device_id=pos, device_id_type=MESH
        )

    pl.semaphore_wait(barrier, 2 + grps - 1 + devs - 1)
    leaf_up = copy(mine.at[1], got.at[0], send_l.at[0], recv_l.at[0], at(above))
    leaf_dn = copy(mine.at[0], got.at[1], send_l.at[1], recv_l.at[1], at(below))
    leaf_up.start()
    leaf_dn.start()

    mg_in.wait()
    for q in range(98):
        m_ref[pl.ds(q, 8, stride=ROWS), 0:98] = mg[q].astype(F32)
    merge = jnp.concatenate([m_ref[ROWS * c : ROWS * c + ROWS, :].astype(BF) for c in range(8)], axis=1)

    def merged(kids):
        x = jnp.concatenate([k.astype(BF) for k in kids], axis=1)
        y = lax.dot_general(x, merge, NT, preferred_element_type=F32)
        return y.astype(BF).astype(F32)

    par_t[:, 0:ROWS] = merged([leaf_t[pl.ds(c, 64, stride=8), :] for c in range(8)])
    gra_t[:, 0:ROWS] = merged([par_t[pl.ds(c, 8, stride=8), :] for c in range(8)])
    msg[...] = jnp.zeros_like(msg)
    msg[:, 0:ROWS] = merged([jnp.broadcast_to(gra_t[c : c + 1, :], (8, 128)) for c in range(8)])

    def send_top(i, c):
        to = lax.rem(g + i, grps)
        copy(msg, buf_a.at[g], send_a.at[i], recv_a.at[g], (to, d)).start()
        return c

    lax.fori_loop(1, grps, send_top, 0)

    both = jnp.concatenate([par_t[...], gra_t[...], jnp.zeros((56, 128), F32)], axis=0)
    midm[...] = both.T[0:112].astype(BF)
    mid_up = copy(midm, midg.at[0], send_m.at[0], recv_m.at[0], at(above))
    mid_dn = copy(midm, midg.at[1], send_m.at[1], recv_m.at[1], at(below))
    mid_up.start()
    mid_dn.start()

    nclass = leaf_lists.shape[0]
    leaf_up.wait()
    leaf_dn.wait()
    w4[...] = jnp.concatenate(
        [b.astype(F32)[0:ROWS] for b in (got[0], mine[0], mine[1], got[1])], axis=0
    ).astype(BF)
    mid_up.wait()
    mid_dn.wait()
    at = lax.broadcasted_iota(jnp.int16, (16, 128), 1)
    for v in range(7):
        rows = slice(16 * v, 16 * v + 16)
        low, own, high = midg[0, rows, :], midm[rows, :], midg[1, rows, :]
        pwin[rows, :] = jnp.where(
            at < 32,
            take_lanes(low, (at + jnp.int16(32)) & jnp.int16(127)),
            jnp.where(
                at < 96,
                take_lanes(own, (at - jnp.int16(32)) & jnp.int16(127)),
                take_lanes(high, (at - jnp.int16(96)) & jnp.int16(127)),
            ),
        )
        gwin[rows, :] = jnp.where(
            at < 4,
            take_lanes(low, (at + jnp.int16(68)) & jnp.int16(127)),
            jnp.where(
                at < 12,
                take_lanes(own, (at + jnp.int16(60)) & jnp.int16(127)),
                take_lanes(high, (at + jnp.int16(52)) & jnp.int16(127)),
            ),
        )
    for r in lists_in:
        r.wait()
    ml_ref[0:64, 0:nclass] = par_l[...]
    ml_ref[64:72, 0:nclass] = gra_l[...]
    mt_ref[0:128, :] = ml_ref[:, 0:128].T
    mt_ref[128:256, :] = ml_ref[:, 128:256].T
    for q in range(98):
        s_ref[pl.ds(q, 8, stride=ROWS), 0:98] = sp[q].astype(F32)

    tr_in.wait()
    sub = lax.broadcasted_iota(jnp.int32, (8, 128), 0)

    def wait_top(i, c):
        frm = lax.rem(g + i, grps)
        w = copy(msg, buf_a.at[frm], send_a.at[i], recv_a.at[frm], (frm, d))
        w.wait_send()
        w.wait_recv()
        return jnp.where(sub == frm, buf_a[frm], c)

    msg_b[...] = lax.fori_loop(1, grps, wait_top, msg[...])

    def send_block(i, c):
        to = lax.rem(d + i, devs)
        copy(msg_b, buf_b.at[d], send_b.at[i], recv_b.at[d], (g, to)).start()
        return c

    lax.fori_loop(1, devs, send_block, 0)
    sub = lax.broadcasted_iota(jnp.int16, (16, 512), 0)
    lane = lax.broadcasted_iota(jnp.int32, (16, 128), 1)

    def leaf_class(row, base):
        lo = jnp.broadcast_to(row & 255, (16, 512)).astype(jnp.int16)
        hi = row >> 8
        onehot = jnp.concatenate(
            [
                jnp.where(lo - jnp.int16(16 * g) == sub, BF(1), BF(0))
                for g in range(16)
            ],
            axis=0,
        )
        r = jnp.dot(w4[...], onehot, preferred_element_type=F32)
        picked = jnp.zeros((ROWS, 512), F32)
        for h in range(4):
            hit = jnp.broadcast_to(hi == h, (ROWS, 512))
            picked = jnp.where(hit, r[h * ROWS : (h + 1) * ROWS], picked)
        g_ref[base : base + ROWS, 0:512] = picked.astype(BF)

    def mid_class(row, base):
        e = jnp.broadcast_to(row, (16, 128))
        lo = (e & 127).astype(jnp.int16)
        is_p = ((lane < 64) & (e >= 0)).astype(jnp.int16) > 0
        is_g = ((lane >= 64) & (lane < 72) & (e >= 0)).astype(jnp.int16) > 0
        for v in range(7):
            rows = slice(16 * v, 16 * v + 16)
            x = jnp.zeros((16, 128), BF)
            x = jnp.where(is_p, take_lanes(pwin[rows, :], lo), x)
            x = jnp.where(is_g, take_lanes(gwin[rows, :], lo), x)
            g_ref[base + 16 * v : base + 16 * v + 16, 512:640] = x

    def group(k0, n):
        for q in range(98):
            a_ref[pl.ds(q, n, stride=ROWS), 0:98] = tr[q, pl.ds(k0, n), :].astype(F32)
        lists = [leaf_lists[pl.ds(k0 + s, min(8, n - s)), :] for s in range(0, n, 8)]
        mids = [mt_ref[pl.ds(k0 + s, min(8, n - s)), :] for s in range(0, n, 8)]
        for c in range(n):
            leaf_class(lists[c // 8][c % 8 : c % 8 + 1], c * 128)
            mid_class(mids[c // 8][c % 8 : c % 8 + 1], c * 128)
        for s in range(0, n, 8):
            m = min(8, n - s)
            ops = jnp.concatenate(
                [a_ref[(s + c) * ROWS : (s + c + 1) * ROWS, :].astype(BF) for c in range(m)], axis=1
            )
            acc_ref[...] += jnp.dot(
                ops, g_ref[s * 128 : (s + m) * 128, :], preferred_element_type=F32
            )

    full = nclass // 16

    def step(j, carry):
        group(pl.multiple_of(j * 16, 16), 16)
        return carry

    lax.fori_loop(0, full, step, 0)
    group(full * 16, nclass - full * 16)

    def wait_block(i, c):
        frm = lax.rem(d + i, devs)
        w = copy(msg_b, buf_b.at[frm], send_b.at[i], recv_b.at[frm], (g, frm))
        w.wait_send()
        w.wait_recv()
        tops[frm] = buf_b[frm]
        return c

    tops[d] = msg_b[...]
    lax.fori_loop(1, devs, wait_block, 0)
    t = top_l[...]
    t = jnp.broadcast_to(jnp.where(t >= 0, (t & 31) * 8 + (t >> 5), -1), (256, nclass))
    hits = jnp.where(lax.broadcasted_iota(jnp.int32, (256, nclass), 0) == t, 1.0, 0.0).astype(BF)
    table = tops[...].reshape(256, 128).astype(BF)
    named = lax.dot_general(hits, table, (((0,), (0,)), ((), ())), preferred_element_type=F32)[:, 0:98]
    for q in range(98):
        tsum_ref[q : q + 1, 0:98] = jnp.sum(tr[q].astype(F32) * named, axis=0, keepdims=True)
    top = jnp.broadcast_to(0.125 * jnp.sum(tsum_ref[...], axis=1, keepdims=True), (ROWS, 128))

    spread = s_ref[...].astype(BF)
    lane = lax.broadcasted_iota(jnp.int32, (ROWS, 128), 1)

    def spread_from(x, index):
        picked = (x if index is None else take_lanes(x, index)).astype(BF)
        z = jnp.dot(
            spread,
            jnp.concatenate([picked, jnp.zeros((128 - ROWS, 128), BF)], axis=0),
            preferred_element_type=F32,
        )
        r = z[0:ROWS]
        for c in range(1, 8):
            r = jnp.where((lane & 7) == c, z[c * ROWS : (c + 1) * ROWS], r)
        return r

    mid = acc_ref[:, 512:640]
    grand = 0.25 * mid + spread_from(top, None)
    parent = 0.5 * mid + spread_from(grand, 64 + ((lane >> 3) & 7))
    for g in range(4):
        cols = slice(128 * g, 128 * g + 128)
        out[:, cols] = (acc_ref[:, cols] + spread_from(parent, 16 * g + (lane >> 3)))[0:98]


def solution(mesh):
    grps, devs = mesh.shape["grp"], mesh.shape["dev"]

    def per_device(
        strengths, source_counts, source_map, merge_ops, translate_ops, spread_ops,
        leaf_lists, parent_lists, grand_lists, top_lists,
    ):
        args = (
            strengths, source_counts.reshape(1, -1), source_map.T, merge_ops.transpose(1, 0, 2),
            leaf_lists, parent_lists.T, grand_lists.T, top_lists.T,
            translate_ops.transpose(1, 0, 2), spread_ops.transpose(1, 0, 2),
        )
        dma = pltpu.SemaphoreType.DMA
        vm = pltpu.VMEM
        return pl.pallas_call(
            lambda *refs: kernel(grps, devs, *refs),
            out_shape=jax.ShapeDtypeStruct((98, leaf_lists.shape[1]), F32),
            in_specs=[pl.BlockSpec(memory_space=pl.ANY)] * len(args),
            out_specs=pl.BlockSpec(memory_space=pltpu.VMEM),
            scratch_shapes=[vm(a.shape, a.dtype) for a in args]
            + [
                vm((8 * ROWS, 128), F32),
                vm((512, 128), F32),
                vm((64, 128), F32),
                vm((8, 128), F32),
                vm((2, 112, 256), BF),
                vm((2, 112, 256), BF),
                vm((112, 128), BF),
                vm((2, 112, 128), BF),
                vm((8, 128), F32),
                vm((grps, 8, 128), F32),
                vm((8, 128), F32),
                vm((devs, 8, 128), F32),
                vm((devs, 8, 128), F32),
                vm((4 * ROWS, 256), BF),
                vm((112, 128), BF),
                vm((112, 128), BF),
                vm((16 * 128, 640), BF),
                vm((16 * ROWS, 128), F32),
                vm((8 * ROWS, 128), F32),
                vm((128, 256), jnp.int32),
                vm((256, 128), jnp.int32),
                vm((ROWS, 640), F32),
                vm((ROWS, 128), F32),
                dma((10,)),
                dma((2,)), dma((2,)), dma((2,)), dma((2,)),
                dma((grps,)), dma((grps,)), dma((devs,)), dma((devs,)),
            ],
            compiler_params=pltpu.CompilerParams(
                collective_id=0, has_side_effects=True, vmem_limit_bytes=48 << 20
            ),
            name="fmm",
        )(*args)

    rows = P(("grp", "dev"))
    cols = P(None, ("grp", "dev"))
    return jax.shard_map(
        per_device,
        mesh=mesh,
        in_specs=(P(("grp", "dev"), None), rows, P(), P(), P(), P(), cols, cols, cols, cols),
        out_specs=cols,
        check_vma=False,
    )
```

```python
import jax
import jax.numpy as jnp
from jax import lax
from jax.experimental import pallas as pl
from jax.experimental.pallas import tpu as pltpu
from jax.sharding import PartitionSpec as P

BF = jnp.bfloat16
F32 = jnp.float32
ROWS = 104
MESH = pl.DeviceIdType.MESH
ZS = 8
LANES = (2, 6, 10, 14)
NT = (((1,), (1,)), ((), ()))


def take_lanes(x, index):
    dims = lax.GatherDimensionNumbers(
        offset_dims=(),
        collapsed_slice_dims=(1,),
        start_index_map=(1,),
        operand_batching_dims=(0,),
        start_indices_batching_dims=(0,),
    )
    return lax.gather(
        x, index[..., None], dims, slice_sizes=(1, 1), mode=lax.GatherScatterMode.PROMISE_IN_BOUNDS
    )


def kernel(
    grps, devs,
    strengths_h, counts_h, smap_h, mg_h, leaf_lists_h, par_h, gra_h, top_h, tr_h, sp_h, out,
    strengths, counts, smap, mg, leaf_lists, par_l, gra_l, top_l, tr, sp,
    m_ref, leaf_t, par_t, gra_t, mine, got, midm, midg, msg, buf_a, msg_b, buf_b, ring, tops,
    w4, win, pwin, gwin, g_ref, a_ref, s_ref, ml_ref, mt_ref, acc_ref, tsum_ref,
    load_sem, send_l, recv_l, send_m, recv_m, send_a, recv_a, send_b, recv_b, send_z, recv_z,
):
    g = lax.axis_index("grp")
    d = lax.axis_index("dev")
    total = grps * devs
    xs = devs // ZS
    x = d // ZS
    me = g * devs + d
    above = lax.rem(me + 1, total)
    below = lax.rem(me + total - 1, total)

    def at(pos):
        return (pos // devs, lax.rem(pos, devs))

    def load(src, dst, k):
        c = pltpu.make_async_copy(src, dst, load_sem.at[k])
        c.start()
        return c

    strengths_in = load(strengths_h, strengths, 0)
    counts_in = load(counts_h, counts, 1)
    smap_in = load(smap_h, smap, 2)
    mg_in = load(mg_h, mg, 3)
    lists_in = [
        load(h, v, 4 + i)
        for i, (h, v) in enumerate(
            ((leaf_lists_h, leaf_lists), (par_h, par_l), (gra_h, gra_l), (top_h, top_l), (sp_h, sp))
        )
    ]
    tr_in = load(tr_h, tr, 9)
    barrier = pltpu.get_barrier_semaphore()

    def greet(pos):
        pl.semaphore_signal(barrier, inc=1, device_id=pos, device_id_type=MESH)

    z = lax.rem(d, ZS)
    first = d - z
    z_up = (g, first + lax.rem(z + 1, ZS))
    z_down = (g, first + lax.rem(z + ZS - 1, ZS))
    greet(at(above))
    greet(at(below))
    greet(z_up)
    greet(z_down)
    lax.fori_loop(1, grps, lambda i, c: (greet((lax.rem(g + i, grps), d)), c)[1], 0)
    lax.fori_loop(1, xs, lambda i, c: (greet((g, lax.rem(d + ZS * i, devs))), c)[1], 0)

    for r in (leaf_t, par_t, gra_t, m_ref, a_ref, s_ref, acc_ref, tsum_ref):
        r[...] = jnp.zeros_like(r)
    g_ref[...] = jnp.zeros_like(g_ref)
    ml_ref[...] = jnp.full_like(ml_ref, -1)
    for r in (strengths_in, counts_in, smap_in):
        r.wait()
    cnt = jnp.concatenate(
        [jnp.broadcast_to(counts[:, 128 * i : 128 * i + 128], (128, 128)).T for i in range(4)], axis=0
    ).astype(jnp.int16)
    slot = lax.broadcasted_iota(jnp.int16, (512, 128), 1)
    zero = jnp.zeros((512, 128), BF)
    live = jnp.concatenate(
        [
            jnp.where(slot < cnt, strengths[:, 0:128], zero),
            jnp.where(slot + jnp.int16(128) < cnt, strengths[:, 128:256], zero),
        ],
        axis=1,
    )
    lt = lax.dot_general(live, smap[...], NT, preferred_element_type=F32)
    leaf_t[:, 0:98] = lt.astype(BF).astype(F32)
    for half in range(2):
        mine[half] = jnp.concatenate(
            [leaf_t[256 * half + 128 * i : 256 * half + 128 * i + 128, :].T[0:112] for i in range(2)], axis=1
        ).astype(BF)

    def copy(src, dst, ss, rs, pos):
        return pltpu.make_async_remote_copy(
            src_ref=src, dst_ref=dst, send_sem=ss, recv_sem=rs, device_id=pos, device_id_type=MESH
        )

    pl.semaphore_wait(barrier, 4 + grps - 1 + xs - 1)
    leaf_up = copy(mine.at[1], got.at[0], send_l.at[0], recv_l.at[0], at(above))
    leaf_dn = copy(mine.at[0], got.at[1], send_l.at[1], recv_l.at[1], at(below))
    leaf_up.start()
    leaf_dn.start()

    mg_in.wait()
    for q in range(98):
        m_ref[pl.ds(q, 8, stride=ROWS), 0:98] = mg[q].astype(F32)
    merge = jnp.concatenate([m_ref[ROWS * c : ROWS * c + ROWS, :].astype(BF) for c in range(8)], axis=1)

    def merged(kids):
        x = jnp.concatenate([k.astype(BF) for k in kids], axis=1)
        y = lax.dot_general(x, merge, NT, preferred_element_type=F32)
        return y.astype(BF).astype(F32)

    par_t[:, 0:ROWS] = merged([leaf_t[pl.ds(c, 64, stride=8), :] for c in range(8)])
    gra_t[:, 0:ROWS] = merged([par_t[pl.ds(c, 8, stride=8), :] for c in range(8)])
    msg[...] = jnp.zeros_like(msg)
    msg[:, 0:ROWS] = merged([jnp.broadcast_to(gra_t[c : c + 1, :], (8, 128)) for c in range(8)])

    def send_top(i, c):
        to = lax.rem(g + i, grps)
        copy(msg, buf_a.at[g], send_a.at[i], recv_a.at[g], (to, d)).start()
        return c

    lax.fori_loop(1, grps, send_top, 0)

    both = jnp.concatenate([par_t[...], gra_t[...], jnp.zeros((56, 128), F32)], axis=0)
    midm[...] = both.T[0:112].astype(BF)
    mid_up = copy(midm, midg.at[0], send_m.at[0], recv_m.at[0], at(above))
    mid_dn = copy(midm, midg.at[1], send_m.at[1], recv_m.at[1], at(below))
    mid_up.start()
    mid_dn.start()

    nclass = leaf_lists.shape[0]
    for r in lists_in:
        r.wait()
    ml_ref[0:64, 0:nclass] = par_l[...]
    ml_ref[64:72, 0:nclass] = gra_l[...]
    mt_ref[0:128, :] = ml_ref[:, 0:128].T
    mt_ref[128:256, :] = ml_ref[:, 128:256].T
    for q in range(98):
        s_ref[pl.ds(q, 8, stride=ROWS), 0:98] = sp[q].astype(F32)
    leaf_up.wait()
    leaf_dn.wait()
    w4[...] = jnp.concatenate(
        [b.astype(F32)[0:ROWS] for b in (got[0], mine[0], mine[1], got[1])], axis=0
    ).astype(BF)
    for h, b in enumerate((got.at[0], mine.at[0], mine.at[1], got.at[1])):
        win[:, 256 * h : 256 * h + 256] = b[...]
    mid_up.wait()
    mid_dn.wait()
    at = lax.broadcasted_iota(jnp.int16, (16, 128), 1)
    for v in range(7):
        rows = slice(16 * v, 16 * v + 16)
        low, own, high = midg[0, rows, :], midm[rows, :], midg[1, rows, :]
        pwin[rows, :] = jnp.where(
            at < 32,
            take_lanes(low, (at + jnp.int16(32)) & jnp.int16(127)),
            jnp.where(
                at < 96,
                take_lanes(own, (at - jnp.int16(32)) & jnp.int16(127)),
                take_lanes(high, (at - jnp.int16(96)) & jnp.int16(127)),
            ),
        )
        gwin[rows, :] = jnp.where(
            at < 4,
            take_lanes(low, (at + jnp.int16(68)) & jnp.int16(127)),
            jnp.where(
                at < 12,
                take_lanes(own, (at + jnp.int16(60)) & jnp.int16(127)),
                take_lanes(high, (at + jnp.int16(52)) & jnp.int16(127)),
            ),
        )
    tr_in.wait()
    sub = lax.broadcasted_iota(jnp.int32, (8, 128), 0)

    def wait_top(i, c):
        frm = lax.rem(g + i, grps)
        w = copy(msg, buf_a.at[frm], send_a.at[i], recv_a.at[frm], (frm, d))
        w.wait_send()
        w.wait_recv()
        return jnp.where(sub == frm, buf_a[frm], c)

    mine_x = lax.fori_loop(1, grps, wait_top, msg[...])
    msg_b[...] = mine_x

    def send_x(i, c):
        copy(msg_b, buf_b.at[x], send_b.at[i], recv_b.at[x], (g, lax.rem(d + ZS * i, devs))).start()
        return c

    lax.fori_loop(1, xs, send_x, 0)

    def wait_x(i, c):
        to = lax.rem(d + ZS * i, devs)
        frm = to // ZS
        w = copy(msg_b, buf_b.at[frm], send_b.at[i], recv_b.at[frm], (g, to))
        w.wait_send()
        w.wait_recv()
        ring[0, 0, frm] = buf_b[frm]
        ring[1, 0, frm] = buf_b[frm]
        return c

    def hops(k):
        return (
            copy(ring.at[0, k], ring.at[0, k + 1], send_z.at[0, k], recv_z.at[0, k + 1], z_up),
            copy(ring.at[1, k], ring.at[1, k + 1], send_z.at[1, k], recv_z.at[1, k + 1], z_down),
        )

    def hop(k):
        @pl.when(k == 0)
        def _():
            ring[0, 0, x] = msg_b[...]
            ring[1, 0, x] = msg_b[...]
            lax.fori_loop(1, xs, wait_x, 0)

        @pl.when(k > 0)
        def _():
            for c in hops(k - 1):
                c.wait()

        for c in hops(k):
            c.start()

    sub = lax.broadcasted_iota(jnp.int16, (16, 512), 0)
    lane = lax.broadcasted_iota(jnp.int32, (16, 128), 1)

    def leaf_class(row, base):
        lo = jnp.broadcast_to(row & 255, (16, 512)).astype(jnp.int16)
        hi = row >> 8
        onehot = jnp.concatenate(
            [
                jnp.where(lo - jnp.int16(16 * g) == sub, BF(1), BF(0))
                for g in range(16)
            ],
            axis=0,
        )
        r = jnp.dot(w4[...], onehot, preferred_element_type=F32)
        picked = jnp.zeros((ROWS, 512), F32)
        for h in range(4):
            hit = jnp.broadcast_to(hi == h, (ROWS, 512))
            picked = jnp.where(hit, r[h * ROWS : (h + 1) * ROWS], picked)
        g_ref[base : base + ROWS, 0:512] = picked.astype(BF)

    def lanes_class(row, base):
        for q in range(4):
            cols = slice(128 * q, 128 * q + 128)
            e = jnp.broadcast_to(row[:, cols], (16, 128))
            lo = (e & 127).astype(jnp.int16)
            hi = (e >> 7).astype(jnp.int16)
            hits = [hi == jnp.int16(b) for b in range(8)]
            for v in range(7):
                rows = slice(16 * v, 16 * v + 16)
                p = jnp.zeros((16, 128), BF)
                for b in range(8):
                    p = jnp.where(hits[b], take_lanes(win[rows, 128 * b : 128 * b + 128], lo), p)
                g_ref[base + 16 * v : base + 16 * v + 16, cols] = p

    def mid_class(row, base):
        e = jnp.broadcast_to(row, (16, 128))
        lo = (e & 127).astype(jnp.int16)
        is_p = ((lane < 64) & (e >= 0)).astype(jnp.int16) > 0
        is_g = ((lane >= 64) & (lane < 72) & (e >= 0)).astype(jnp.int16) > 0
        for v in range(7):
            rows = slice(16 * v, 16 * v + 16)
            x = jnp.zeros((16, 128), BF)
            x = jnp.where(is_p, take_lanes(pwin[rows, :], lo), x)
            x = jnp.where(is_g, take_lanes(gwin[rows, :], lo), x)
            g_ref[base + 16 * v : base + 16 * v + 16, 512:640] = x

    def group(k0, n):
        for q in range(98):
            a_ref[pl.ds(q, n, stride=ROWS), 0:98] = tr[q, pl.ds(k0, n), :].astype(F32)
        lists = [leaf_lists[pl.ds(k0 + s, min(8, n - s)), :] for s in range(0, n, 8)]
        mids = [mt_ref[pl.ds(k0 + s, min(8, n - s)), :] for s in range(0, n, 8)]
        for c in range(n):
            pick = lanes_class if c in LANES else leaf_class
            pick(lists[c // 8][c % 8 : c % 8 + 1], c * 128)
            mid_class(mids[c // 8][c % 8 : c % 8 + 1], c * 128)
        for s in range(0, n, 8):
            m = min(8, n - s)
            ops = jnp.concatenate(
                [a_ref[(s + c) * ROWS : (s + c + 1) * ROWS, :].astype(BF) for c in range(m)], axis=1
            )
            acc_ref[...] += jnp.dot(
                ops, g_ref[s * 128 : (s + m) * 128, :], preferred_element_type=F32
            )

    full = nclass // 16

    def step(j, carry):
        @pl.when((lax.rem(j, 2) == 1) & (j < ZS))
        def _():
            hop(j // 2)

        group(pl.multiple_of(j * 16, 16), 16)
        return carry

    lax.fori_loop(0, full, step, 0)
    group(full * 16, nclass - full * 16)

    for c in hops(ZS // 2 - 1):
        c.wait()
    for k in range(ZS // 2 + 1):
        tops[lax.rem(z + ZS - k, ZS)] = ring[0, k]
    for k in range(1, ZS // 2):
        tops[lax.rem(z + k, ZS)] = ring[1, k]
    t = top_l[...]
    t = jnp.broadcast_to(jnp.where(t >= 0, (t & 7) * 32 + (t & 24) + (t >> 5), -1), (256, nclass))
    hits = jnp.where(lax.broadcasted_iota(jnp.int32, (256, nclass), 0) == t, 1.0, 0.0).astype(BF)
    table = tops[...].reshape(256, 128).astype(BF)
    named = lax.dot_general(hits, table, (((0,), (0,)), ((), ())), preferred_element_type=F32)[:, 0:98]
    for q in range(98):
        tsum_ref[q : q + 1, 0:98] = jnp.sum(tr[q].astype(F32) * named, axis=0, keepdims=True)
    top = jnp.broadcast_to(0.125 * jnp.sum(tsum_ref[...], axis=1, keepdims=True), (ROWS, 128))

    spread = s_ref[...].astype(BF)
    lane = lax.broadcasted_iota(jnp.int32, (ROWS, 128), 1)

    def spread_from(x, index):
        picked = (x if index is None else take_lanes(x, index)).astype(BF)
        z = jnp.dot(
            spread,
            jnp.concatenate([picked, jnp.zeros((128 - ROWS, 128), BF)], axis=0),
            preferred_element_type=F32,
        )
        r = z[0:ROWS]
        for c in range(1, 8):
            r = jnp.where((lane & 7) == c, z[c * ROWS : (c + 1) * ROWS], r)
        return r

    mid = acc_ref[:, 512:640]
    grand = 0.25 * mid + spread_from(top, None)
    parent = 0.5 * mid + spread_from(grand, 64 + ((lane >> 3) & 7))
    for g in range(4):
        cols = slice(128 * g, 128 * g + 128)
        out[:, cols] = (acc_ref[:, cols] + spread_from(parent, 16 * g + (lane >> 3)))[0:98]


def solution(mesh):
    grps, devs = mesh.shape["grp"], mesh.shape["dev"]

    def per_device(
        strengths, source_counts, source_map, merge_ops, translate_ops, spread_ops,
        leaf_lists, parent_lists, grand_lists, top_lists,
    ):
        args = (
            strengths, source_counts.reshape(1, -1), source_map.T, merge_ops.transpose(1, 0, 2),
            leaf_lists, parent_lists.T, grand_lists.T, top_lists.T,
            translate_ops.transpose(1, 0, 2), spread_ops.transpose(1, 0, 2),
        )
        dma = pltpu.SemaphoreType.DMA
        vm = pltpu.VMEM
        return pl.pallas_call(
            lambda *refs: kernel(grps, devs, *refs),
            out_shape=jax.ShapeDtypeStruct((98, leaf_lists.shape[1]), F32),
            in_specs=[pl.BlockSpec(memory_space=pl.ANY)] * len(args),
            out_specs=pl.BlockSpec(memory_space=pltpu.VMEM),
            scratch_shapes=[vm(a.shape, a.dtype) for a in args]
            + [
                vm((8 * ROWS, 128), F32),
                vm((512, 128), F32),
                vm((64, 128), F32),
                vm((8, 128), F32),
                vm((2, 112, 256), BF),
                vm((2, 112, 256), BF),
                vm((112, 128), BF),
                vm((2, 112, 128), BF),
                vm((8, 128), F32),
                vm((grps, 8, 128), F32),
                vm((8, 128), F32),
                vm((devs // ZS, 8, 128), F32),
                vm((2, ZS // 2 + 1, devs // ZS, 8, 128), F32),
                vm((ZS, devs // ZS, grps, 128), F32),
                vm((4 * ROWS, 256), BF),
                vm((112, 1024), BF),
                vm((112, 128), BF),
                vm((112, 128), BF),
                vm((16 * 128, 640), BF),
                vm((16 * ROWS, 128), F32),
                vm((8 * ROWS, 128), F32),
                vm((128, 256), jnp.int32),
                vm((256, 128), jnp.int32),
                vm((ROWS, 640), F32),
                vm((ROWS, 128), F32),
                dma((10,)),
                dma((2,)), dma((2,)), dma((2,)), dma((2,)),
                dma((grps,)), dma((grps,)), dma((devs // ZS,)), dma((devs // ZS,)),
                dma((2, ZS // 2 + 1)), dma((2, ZS // 2 + 1)),
            ],
            compiler_params=pltpu.CompilerParams(
                collective_id=0, has_side_effects=True, vmem_limit_bytes=60 << 20
            ),
            name="fmm",
        )(*args)

    rows = P(("grp", "dev"))
    cols = P(None, ("grp", "dev"))
    return jax.shard_map(
        per_device,
        mesh=mesh,
        in_specs=(P(("grp", "dev"), None), rows, P(), P(), P(), P(), cols, cols, cols, cols),
        out_specs=cols,
        check_vma=False,
    )
```

```python
import jax
import jax.numpy as jnp
from jax import lax
from jax.experimental import pallas as pl
from jax.experimental.pallas import tpu as pltpu
from jax.sharding import PartitionSpec as P

BF = jnp.bfloat16
F32 = jnp.float32
ROWS = 104
MESH = pl.DeviceIdType.MESH
ZS = 8
LANES = (2, 6, 10, 14)
EARLY = 4
NT = (((1,), (1,)), ((), ()))


def take_lanes(x, index):
    dims = lax.GatherDimensionNumbers(
        offset_dims=(),
        collapsed_slice_dims=(1,),
        start_index_map=(1,),
        operand_batching_dims=(0,),
        start_indices_batching_dims=(0,),
    )
    return lax.gather(
        x, index[..., None], dims, slice_sizes=(1, 1), mode=lax.GatherScatterMode.PROMISE_IN_BOUNDS
    )


def kernel(
    grps, devs,
    strengths_h, counts_h, smap_h, mg_h, leaf_lists_h, par_h, gra_h, top_h, tr_h, sp_h, out,
    strengths, counts, smap, mg, leaf_lists, par_l, gra_l, top_l, tr, sp,
    m_ref, leaf_t, par_t, gra_t, mine, got, midm, midg, msg, buf_a, msg_b, buf_b, ring, tops,
    w4, win, pwin, gwin, go_ref, g_ref, a_ref, s_ref, ml_ref, mt_ref, acc_ref, tsum_ref,
    load_sem, send_l, recv_l, send_m, recv_m, send_a, recv_a, send_b, recv_b, send_z, recv_z,
):
    g = lax.axis_index("grp")
    d = lax.axis_index("dev")
    total = grps * devs
    xs = devs // ZS
    x = d // ZS
    me = g * devs + d
    above = lax.rem(me + 1, total)
    below = lax.rem(me + total - 1, total)

    def at(pos):
        return (pos // devs, lax.rem(pos, devs))

    def load(src, dst, k):
        c = pltpu.make_async_copy(src, dst, load_sem.at[k])
        c.start()
        return c

    strengths_in = load(strengths_h, strengths, 0)
    counts_in = load(counts_h, counts, 1)
    smap_in = load(smap_h, smap, 2)
    mg_in = load(mg_h, mg, 3)
    lists_in = [
        load(h, v, 4 + i)
        for i, (h, v) in enumerate(
            ((leaf_lists_h, leaf_lists), (par_h, par_l), (gra_h, gra_l), (top_h, top_l), (sp_h, sp))
        )
    ]
    tr_in = load(tr_h, tr, 9)
    barrier = pltpu.get_barrier_semaphore()

    def greet(pos):
        pl.semaphore_signal(barrier, inc=1, device_id=pos, device_id_type=MESH)

    z = lax.rem(d, ZS)
    first = d - z
    z_up = (g, first + lax.rem(z + 1, ZS))
    z_down = (g, first + lax.rem(z + ZS - 1, ZS))
    greet(at(above))
    greet(at(below))
    greet(z_up)
    greet(z_down)
    lax.fori_loop(1, grps, lambda i, c: (greet((lax.rem(g + i, grps), d)), c)[1], 0)
    lax.fori_loop(1, xs, lambda i, c: (greet((g, lax.rem(d + ZS * i, devs))), c)[1], 0)

    for r in (leaf_t, par_t, gra_t, m_ref, a_ref, s_ref, acc_ref, tsum_ref):
        r[...] = jnp.zeros_like(r)
    g_ref[...] = jnp.zeros_like(g_ref)
    ml_ref[...] = jnp.full_like(ml_ref, -1)
    for r in (strengths_in, counts_in, smap_in):
        r.wait()
    cnt = jnp.concatenate(
        [jnp.broadcast_to(counts[:, 128 * i : 128 * i + 128], (128, 128)).T for i in range(4)], axis=0
    ).astype(jnp.int16)
    slot = lax.broadcasted_iota(jnp.int16, (512, 128), 1)
    zero = jnp.zeros((512, 128), BF)
    live = jnp.concatenate(
        [
            jnp.where(slot < cnt, strengths[:, 0:128], zero),
            jnp.where(slot + jnp.int16(128) < cnt, strengths[:, 128:256], zero),
        ],
        axis=1,
    )
    lt = lax.dot_general(live, smap[...], NT, preferred_element_type=F32)
    leaf_t[:, 0:98] = lt.astype(BF).astype(F32)
    for half in range(2):
        mine[half] = jnp.concatenate(
            [leaf_t[256 * half + 128 * i : 256 * half + 128 * i + 128, :].T[0:112] for i in range(2)], axis=1
        ).astype(BF)

    def copy(src, dst, ss, rs, pos):
        return pltpu.make_async_remote_copy(
            src_ref=src, dst_ref=dst, send_sem=ss, recv_sem=rs, device_id=pos, device_id_type=MESH
        )

    pl.semaphore_wait(barrier, 4 + grps - 1 + xs - 1)
    leaf_up = copy(mine.at[1], got.at[0], send_l.at[0], recv_l.at[0], at(above))
    leaf_dn = copy(mine.at[0], got.at[1], send_l.at[1], recv_l.at[1], at(below))
    leaf_up.start()
    leaf_dn.start()

    mg_in.wait()
    for q in range(98):
        m_ref[pl.ds(q, 8, stride=ROWS), 0:98] = mg[q].astype(F32)
    merge = jnp.concatenate([m_ref[ROWS * c : ROWS * c + ROWS, :].astype(BF) for c in range(8)], axis=1)

    def merged(kids):
        x = jnp.concatenate([k.astype(BF) for k in kids], axis=1)
        y = lax.dot_general(x, merge, NT, preferred_element_type=F32)
        return y.astype(BF).astype(F32)

    par_t[:, 0:ROWS] = merged([leaf_t[pl.ds(c, 64, stride=8), :] for c in range(8)])
    gra_t[:, 0:ROWS] = merged([par_t[pl.ds(c, 8, stride=8), :] for c in range(8)])
    msg[...] = jnp.zeros_like(msg)
    msg[:, 0:ROWS] = merged([jnp.broadcast_to(gra_t[c : c + 1, :], (8, 128)) for c in range(8)])

    def send_top(i, c):
        to = lax.rem(g + i, grps)
        copy(msg, buf_a.at[g], send_a.at[i], recv_a.at[g], (to, d)).start()
        return c

    lax.fori_loop(1, grps, send_top, 0)

    both = jnp.concatenate([par_t[...], gra_t[...], jnp.zeros((56, 128), F32)], axis=0)
    midm[...] = both.T[0:112].astype(BF)
    mid_up = copy(midm, midg.at[0], send_m.at[0], recv_m.at[0], at(above))
    mid_dn = copy(midm, midg.at[1], send_m.at[1], recv_m.at[1], at(below))
    mid_up.start()
    mid_dn.start()

    nclass = leaf_lists.shape[0]
    for r in lists_in:
        r.wait()
    ml_ref[0:64, 0:nclass] = par_l[...]
    ml_ref[64:72, 0:nclass] = gra_l[...]
    mt_ref[0:128, :] = ml_ref[:, 0:128].T
    mt_ref[128:256, :] = ml_ref[:, 128:256].T
    for q in range(98):
        s_ref[pl.ds(q, 8, stride=ROWS), 0:98] = sp[q].astype(F32)
    sub8 = lax.broadcasted_iota(jnp.int32, (8, 128), 0)

    def wait_top(i, c):
        frm = lax.rem(g + i, grps)
        w = copy(msg, buf_a.at[frm], send_a.at[i], recv_a.at[frm], (frm, d))
        w.wait_send()
        w.wait_recv()
        return jnp.where(sub8 == frm, buf_a[frm], c)

    def send_x(i, c):
        copy(msg_b, buf_b.at[x], send_b.at[i], recv_b.at[x], (g, lax.rem(d + ZS * i, devs))).start()
        return c

    def pass_x():
        msg_b[...] = lax.fori_loop(1, grps, wait_top, msg[...])
        lax.fori_loop(1, xs, send_x, 0)

    def wait_x(i, c):
        to = lax.rem(d + ZS * i, devs)
        frm = to // ZS
        w = copy(msg_b, buf_b.at[frm], send_b.at[i], recv_b.at[frm], (g, to))
        w.wait_send()
        w.wait_recv()
        ring[0, 0, frm] = buf_b[frm]
        ring[1, 0, frm] = buf_b[frm]
        return c

    def hops(k):
        return (
            copy(ring.at[0, k], ring.at[0, k + 1], send_z.at[0, k], recv_z.at[0, k + 1], z_up),
            copy(ring.at[1, k], ring.at[1, k + 1], send_z.at[1, k], recv_z.at[1, k + 1], z_down),
        )

    def hop_first():
        ring[0, 0, x] = msg_b[...]
        ring[1, 0, x] = msg_b[...]
        lax.fori_loop(1, xs, wait_x, 0)
        for c in hops(0):
            c.start()

    def hop_next(k):
        for c in hops(k - 1):
            c.wait()
        for c in hops(k):
            c.start()

    sub = lax.broadcasted_iota(jnp.int16, (16, 512), 0)
    lane = lax.broadcasted_iota(jnp.int32, (16, 128), 1)

    def place(slot, blocks, parts):
        w4[slot * ROWS : (slot + 2) * ROWS, :] = jnp.concatenate(
            [p[...].astype(F32)[0:ROWS] for p in parts], axis=0
        ).astype(BF)
        for h, p in zip(blocks, parts):
            win[:, 256 * h : 256 * h + 256] = p[...]

    def leaf_class(row, old, new, blocks):
        lo = jnp.broadcast_to(row & 255, (16, 512)).astype(jnp.int16)
        hi = row >> 8
        onehot = jnp.concatenate(
            [jnp.where(lo - jnp.int16(16 * i) == sub, BF(1), BF(0)) for i in range(16)], axis=0
        )
        at0 = 2 * ROWS if blocks[0] == 0 else 0
        r = jnp.dot(w4[at0 : at0 + len(blocks) * ROWS, :], onehot, preferred_element_type=F32)
        picked = jnp.zeros((ROWS, 512), F32) if old is None else old[0:ROWS, :].astype(F32)
        for i, h in enumerate(blocks):
            hit = jnp.broadcast_to(hi == h, (ROWS, 512))
            picked = jnp.where(hit, r[i * ROWS : (i + 1) * ROWS], picked)
        new[0:ROWS, 0:512] = picked.astype(BF)

    def lanes_class(row, old, new, blocks):
        for i in range(4):
            cols = slice(128 * i, 128 * i + 128)
            e = jnp.broadcast_to(row[:, cols], (16, 128))
            lo = (e & 127).astype(jnp.int16)
            hi = (e >> 7).astype(jnp.int16)
            sources = [b for h in blocks for b in (2 * h, 2 * h + 1)]
            hits = [hi == jnp.int16(b) for b in sources]
            for v in range(7):
                rows = slice(16 * v, 16 * v + 16)
                p = jnp.zeros((16, 128), BF) if old is None else old[rows, cols]
                for hit, b in zip(hits, sources):
                    p = jnp.where(hit, take_lanes(win[rows, 128 * b : 128 * b + 128], lo), p)
                new[rows, cols] = p

    def mid_class(row, base):
        e = jnp.broadcast_to(row, (16, 128))
        lo = (e & 127).astype(jnp.int16)
        is_p = ((lane < 64) & (e >= 0)).astype(jnp.int16) > 0
        is_g = ((lane >= 64) & (lane < 72) & (e >= 0)).astype(jnp.int16) > 0
        for v in range(7):
            rows = slice(16 * v, 16 * v + 16)
            x = jnp.zeros((16, 128), BF)
            x = jnp.where(is_p, take_lanes(pwin[rows, :], lo), x)
            x = jnp.where(is_g, take_lanes(gwin[rows, :], lo), x)
            g_ref[base + 16 * v : base + 16 * v + 16, 512:640] = x

    def lists_of(k0, n):
        lists = [leaf_lists[pl.ds(k0 + i, min(8, n - i)), :] for i in range(0, n, 8)]
        return [lists[c // 8][c % 8 : c % 8 + 1] for c in range(n)]

    def pick(c, *rest):
        (lanes_class if c in LANES else leaf_class)(*rest)

    def own_group(j):
        rows = lists_of(pl.multiple_of(j * 16, 16), 16)
        for c in range(16):
            pick(c, rows[c], None, go_ref.at[j, pl.ds(c * 128, 128), :], (1, 2))

    def group(k0, n, early=None):
        rows = lists_of(k0, n)
        mids = [mt_ref[pl.ds(k0 + i, min(8, n - i)), :] for i in range(0, n, 8)]
        for q in range(98):
            a_ref[pl.ds(q, n, stride=ROWS), 0:98] = tr[q, pl.ds(k0, n), :].astype(F32)
        for c in range(n):
            new = g_ref.at[pl.ds(c * 128, 128), :]
            if early is None:
                pick(c, rows[c], None, new, (1, 2, 0, 3))
            else:
                pick(c, rows[c], go_ref.at[early, pl.ds(c * 128, 128), :], new, (0, 3))
            mid_class(mids[c // 8][c % 8 : c % 8 + 1], c * 128)
        for i in range(0, n, 8):
            m = min(8, n - i)
            ops = jnp.concatenate(
                [a_ref[(i + c) * ROWS : (i + c + 1) * ROWS, :].astype(BF) for c in range(m)], axis=1
            )
            acc_ref[...] += jnp.dot(
                ops, g_ref[i * 128 : (i + m) * 128, :], preferred_element_type=F32
            )

    place(0, (1, 2), (mine.at[0], mine.at[1]))
    lax.fori_loop(0, EARLY, lambda j, c: (own_group(j), c)[1], 0)
    leaf_up.wait()
    leaf_dn.wait()
    place(2, (0, 3), (got.at[0], got.at[1]))
    mid_up.wait()
    mid_dn.wait()
    at = lax.broadcasted_iota(jnp.int16, (16, 128), 1)
    for v in range(7):
        rows = slice(16 * v, 16 * v + 16)
        low, own, high = midg[0, rows, :], midm[rows, :], midg[1, rows, :]
        pwin[rows, :] = jnp.where(
            at < 32,
            take_lanes(low, (at + jnp.int16(32)) & jnp.int16(127)),
            jnp.where(
                at < 96,
                take_lanes(own, (at - jnp.int16(32)) & jnp.int16(127)),
                take_lanes(high, (at - jnp.int16(96)) & jnp.int16(127)),
            ),
        )
        gwin[rows, :] = jnp.where(
            at < 4,
            take_lanes(low, (at + jnp.int16(68)) & jnp.int16(127)),
            jnp.where(
                at < 12,
                take_lanes(own, (at + jnp.int16(60)) & jnp.int16(127)),
                take_lanes(high, (at + jnp.int16(52)) & jnp.int16(127)),
            ),
        )
    tr_in.wait()

    def late_step(j, carry):
        @pl.when(j == 0)
        def _():
            pass_x()

        @pl.when(j == 2)
        def _():
            hop_first()

        group(pl.multiple_of(j * 16, 16), 16, j)
        return carry

    def step(j, carry):
        k = (j - EARLY + 2) // 2

        @pl.when((lax.rem(j - EARLY, 2) == 0) & (k < ZS // 2))
        def _():
            hop_next(k)

        group(pl.multiple_of(j * 16, 16), 16)
        return carry

    full = nclass // 16
    lax.fori_loop(0, EARLY, late_step, 0)
    lax.fori_loop(EARLY, full, step, 0)
    for c in hops(ZS // 2 - 1):
        c.wait()
    for k in range(ZS // 2 + 1):
        tops[lax.rem(z + ZS - k, ZS)] = ring[0, k]
    for k in range(1, ZS // 2):
        tops[lax.rem(z + k, ZS)] = ring[1, k]
    t = top_l[...]
    t = jnp.broadcast_to(jnp.where(t >= 0, (t & 7) * 32 + (t & 24) + (t >> 5), -1), (256, nclass))
    hits = jnp.where(lax.broadcasted_iota(jnp.int32, (256, nclass), 0) == t, 1.0, 0.0).astype(BF)
    table = tops[...].reshape(256, 128).astype(BF)
    named = lax.dot_general(hits, table, (((0,), (0,)), ((), ())), preferred_element_type=F32)[:, 0:98]
    for q in range(98):
        tsum_ref[q : q + 1, 0:98] = jnp.sum(tr[q].astype(F32) * named, axis=0, keepdims=True)
    top = jnp.broadcast_to(0.125 * jnp.sum(tsum_ref[...], axis=1, keepdims=True), (ROWS, 128))
    group(full * 16, nclass - full * 16)

    spread = s_ref[...].astype(BF)
    lane = lax.broadcasted_iota(jnp.int32, (ROWS, 128), 1)

    def spread_from(x, index):
        picked = (x if index is None else take_lanes(x, index)).astype(BF)
        z = jnp.dot(
            spread,
            jnp.concatenate([picked, jnp.zeros((128 - ROWS, 128), BF)], axis=0),
            preferred_element_type=F32,
        )
        r = z[0:ROWS]
        for c in range(1, 8):
            r = jnp.where((lane & 7) == c, z[c * ROWS : (c + 1) * ROWS], r)
        return r

    mid = acc_ref[:, 512:640]
    grand = 0.25 * mid + spread_from(top, None)
    parent = 0.5 * mid + spread_from(grand, 64 + ((lane >> 3) & 7))
    for g in range(4):
        cols = slice(128 * g, 128 * g + 128)
        out[:, cols] = (acc_ref[:, cols] + spread_from(parent, 16 * g + (lane >> 3)))[0:98]


def solution(mesh):
    grps, devs = mesh.shape["grp"], mesh.shape["dev"]

    def per_device(
        strengths, source_counts, source_map, merge_ops, translate_ops, spread_ops,
        leaf_lists, parent_lists, grand_lists, top_lists,
    ):
        args = (
            strengths, source_counts.reshape(1, -1), source_map.T, merge_ops.transpose(1, 0, 2),
            leaf_lists, parent_lists.T, grand_lists.T, top_lists.T,
            translate_ops.transpose(1, 0, 2), spread_ops.transpose(1, 0, 2),
        )
        dma = pltpu.SemaphoreType.DMA
        vm = pltpu.VMEM
        return pl.pallas_call(
            lambda *refs: kernel(grps, devs, *refs),
            out_shape=jax.ShapeDtypeStruct((98, leaf_lists.shape[1]), F32),
            in_specs=[pl.BlockSpec(memory_space=pl.ANY)] * len(args),
            out_specs=pl.BlockSpec(memory_space=pltpu.VMEM),
            scratch_shapes=[vm(a.shape, a.dtype) for a in args]
            + [
                vm((8 * ROWS, 128), F32),
                vm((512, 128), F32),
                vm((64, 128), F32),
                vm((8, 128), F32),
                vm((2, 112, 256), BF),
                vm((2, 112, 256), BF),
                vm((112, 128), BF),
                vm((2, 112, 128), BF),
                vm((8, 128), F32),
                vm((grps, 8, 128), F32),
                vm((8, 128), F32),
                vm((devs // ZS, 8, 128), F32),
                vm((2, ZS // 2 + 1, devs // ZS, 8, 128), F32),
                vm((ZS, devs // ZS, grps, 128), F32),
                vm((4 * ROWS, 256), BF),
                vm((112, 1024), BF),
                vm((112, 128), BF),
                vm((112, 128), BF),
                vm((EARLY, 16 * 128, 512), BF),
                vm((16 * 128, 640), BF),
                vm((16 * ROWS, 128), F32),
                vm((8 * ROWS, 128), F32),
                vm((128, 256), jnp.int32),
                vm((256, 128), jnp.int32),
                vm((ROWS, 640), F32),
                vm((ROWS, 128), F32),
                dma((10,)),
                dma((2,)), dma((2,)), dma((2,)), dma((2,)),
                dma((grps,)), dma((grps,)), dma((devs // ZS,)), dma((devs // ZS,)),
                dma((2, ZS // 2 + 1)), dma((2, ZS // 2 + 1)),
            ],
            compiler_params=pltpu.CompilerParams(
                collective_id=0, has_side_effects=True, vmem_limit_bytes=60 << 20
            ),
            name="fmm",
        )(*args)

    rows = P(("grp", "dev"))
    cols = P(None, ("grp", "dev"))
    return jax.shard_map(
        per_device,
        mesh=mesh,
        in_specs=(P(("grp", "dev"), None), rows, P(), P(), P(), P(), cols, cols, cols, cols),
        out_specs=cols,
        check_vma=False,
    )
```

```python
import jax
import jax.numpy as jnp
from jax import lax
from jax.experimental import pallas as pl
from jax.experimental.pallas import tpu as pltpu
from jax.sharding import PartitionSpec as P

BF = jnp.bfloat16
F32 = jnp.float32
ROWS = 104
MESH = pl.DeviceIdType.MESH
ZS = 8
LANES = (2, 6, 10, 14)
EARLY = 7
NT = (((1,), (1,)), ((), ()))


def take_lanes(x, index):
    dims = lax.GatherDimensionNumbers(
        offset_dims=(),
        collapsed_slice_dims=(1,),
        start_index_map=(1,),
        operand_batching_dims=(0,),
        start_indices_batching_dims=(0,),
    )
    return lax.gather(
        x, index[..., None], dims, slice_sizes=(1, 1), mode=lax.GatherScatterMode.PROMISE_IN_BOUNDS
    )


def kernel(
    grps, devs,
    strengths_h, counts_h, smap_h, mg_h, leaf_lists_h, par_h, gra_h, top_h, tr_h, sp_h, out,
    strengths, counts, smap, mg, leaf_lists, par_l, gra_l, top_l, tr, sp,
    m_ref, leaf_t, par_t, gra_t, mine, got, midm, midg, msg, buf_a, msg_b, buf_b, ring, tops,
    w4, win, pwin, gwin, go_ref, g_ref, a_ref, s_ref, ml_ref, mt_ref, acc_ref, tsum_ref,
    load_sem, send_l, recv_l, send_m, recv_m, send_a, recv_a, send_b, recv_b, send_z, recv_z,
):
    g = lax.axis_index("grp")
    d = lax.axis_index("dev")
    total = grps * devs
    xs = devs // ZS
    x = d // ZS
    me = g * devs + d
    above = lax.rem(me + 1, total)
    below = lax.rem(me + total - 1, total)

    def at(pos):
        return (pos // devs, lax.rem(pos, devs))

    def load(src, dst, k):
        c = pltpu.make_async_copy(src, dst, load_sem.at[k])
        c.start()
        return c

    strengths_in = load(strengths_h, strengths, 0)
    counts_in = load(counts_h, counts, 1)
    smap_in = load(smap_h, smap, 2)
    mg_in = load(mg_h, mg, 3)
    lists_in = [
        load(h, v, 4 + i)
        for i, (h, v) in enumerate(
            ((leaf_lists_h, leaf_lists), (par_h, par_l), (gra_h, gra_l), (top_h, top_l), (sp_h, sp))
        )
    ]
    tr_in = load(tr_h, tr, 9)
    barrier = pltpu.get_barrier_semaphore()

    def greet(pos):
        pl.semaphore_signal(barrier, inc=1, device_id=pos, device_id_type=MESH)

    z = lax.rem(d, ZS)
    first = d - z
    z_up = (g, first + lax.rem(z + 1, ZS))
    z_down = (g, first + lax.rem(z + ZS - 1, ZS))
    greet(at(above))
    greet(at(below))
    greet(z_up)
    greet(z_down)
    lax.fori_loop(1, grps, lambda i, c: (greet((lax.rem(g + i, grps), d)), c)[1], 0)
    lax.fori_loop(1, xs, lambda i, c: (greet((g, lax.rem(d + ZS * i, devs))), c)[1], 0)

    for r in (leaf_t, par_t, gra_t, m_ref, a_ref, s_ref, acc_ref, tsum_ref):
        r[...] = jnp.zeros_like(r)
    g_ref[...] = jnp.zeros_like(g_ref)
    ml_ref[...] = jnp.full_like(ml_ref, -1)
    for r in (strengths_in, counts_in, smap_in):
        r.wait()
    cnt = jnp.concatenate(
        [jnp.broadcast_to(counts[:, 128 * i : 128 * i + 128], (128, 128)).T for i in range(4)], axis=0
    ).astype(jnp.int16)
    slot = lax.broadcasted_iota(jnp.int16, (512, 128), 1)
    zero = jnp.zeros((512, 128), BF)
    live = jnp.concatenate(
        [
            jnp.where(slot < cnt, strengths[:, 0:128], zero),
            jnp.where(slot + jnp.int16(128) < cnt, strengths[:, 128:256], zero),
        ],
        axis=1,
    )
    lt = lax.dot_general(live, smap[...], NT, preferred_element_type=F32)
    leaf_t[:, 0:98] = lt.astype(BF).astype(F32)
    for half in range(2):
        mine[half] = jnp.concatenate(
            [leaf_t[256 * half + 128 * i : 256 * half + 128 * i + 128, :].T[0:112] for i in range(2)], axis=1
        ).astype(BF)

    def copy(src, dst, ss, rs, pos):
        return pltpu.make_async_remote_copy(
            src_ref=src, dst_ref=dst, send_sem=ss, recv_sem=rs, device_id=pos, device_id_type=MESH
        )

    sub = lax.broadcasted_iota(jnp.int16, (16, 512), 0)
    lane = lax.broadcasted_iota(jnp.int32, (16, 128), 1)

    def place(slot, blocks, parts):
        w4[slot * ROWS : (slot + 2) * ROWS, :] = jnp.concatenate(
            [p[...].astype(F32)[0:ROWS] for p in parts], axis=0
        ).astype(BF)
        for h, p in zip(blocks, parts):
            win[:, 256 * h : 256 * h + 256] = p[...]

    def leaf_class(row, old, new, blocks):
        lo = jnp.broadcast_to(row & 255, (16, 512)).astype(jnp.int16)
        hi = row >> 8
        onehot = jnp.concatenate(
            [jnp.where(lo - jnp.int16(16 * i) == sub, BF(1), BF(0)) for i in range(16)], axis=0
        )
        at0 = 2 * ROWS if blocks[0] == 0 else 0
        r = jnp.dot(w4[at0 : at0 + len(blocks) * ROWS, :], onehot, preferred_element_type=F32)
        picked = jnp.zeros((ROWS, 512), F32) if old is None else old[0:ROWS, :].astype(F32)
        for i, h in enumerate(blocks):
            hit = jnp.broadcast_to(hi == h, (ROWS, 512))
            picked = jnp.where(hit, r[i * ROWS : (i + 1) * ROWS], picked)
        new[0:ROWS, 0:512] = picked.astype(BF)

    def lanes_class(row, old, new, blocks):
        for i in range(4):
            cols = slice(128 * i, 128 * i + 128)
            e = jnp.broadcast_to(row[:, cols], (16, 128))
            lo = (e & 127).astype(jnp.int16)
            hi = (e >> 7).astype(jnp.int16)
            sources = [b for h in blocks for b in (2 * h, 2 * h + 1)]
            hits = [hi == jnp.int16(b) for b in sources]
            for v in range(7):
                rows = slice(16 * v, 16 * v + 16)
                p = jnp.zeros((16, 128), BF) if old is None else old[rows, cols]
                for hit, b in zip(hits, sources):
                    p = jnp.where(hit, take_lanes(win[rows, 128 * b : 128 * b + 128], lo), p)
                new[rows, cols] = p

    def lists_of(k0, n):
        lists = [leaf_lists[pl.ds(k0 + i, min(8, n - i)), :] for i in range(0, n, 8)]
        return [lists[c // 8][c % 8 : c % 8 + 1] for c in range(n)]

    def pick(c, *rest):
        (lanes_class if c in LANES else leaf_class)(*rest)

    def own_group(j):
        rows = lists_of(pl.multiple_of(j * 16, 16), 16)
        for c in range(16):
            pick(c, rows[c], None, go_ref.at[j, pl.ds(c * 128, 128), :], (1, 2))

    place(0, (1, 2), (mine.at[0], mine.at[1]))
    lists_in[0].wait()
    ahead = jnp.where(z == 0, 4, jnp.where(z == 1, 2, 0))
    lax.fori_loop(0, ahead, lambda j, c: (own_group(j), c)[1], 0)
    pl.semaphore_wait(barrier, 4 + grps - 1 + xs - 1)
    leaf_up = copy(mine.at[1], got.at[0], send_l.at[0], recv_l.at[0], at(above))
    leaf_dn = copy(mine.at[0], got.at[1], send_l.at[1], recv_l.at[1], at(below))
    leaf_up.start()
    leaf_dn.start()

    mg_in.wait()
    for q in range(98):
        m_ref[pl.ds(q, 8, stride=ROWS), 0:98] = mg[q].astype(F32)
    merge = jnp.concatenate([m_ref[ROWS * c : ROWS * c + ROWS, :].astype(BF) for c in range(8)], axis=1)

    def merged(kids):
        x = jnp.concatenate([k.astype(BF) for k in kids], axis=1)
        y = lax.dot_general(x, merge, NT, preferred_element_type=F32)
        return y.astype(BF).astype(F32)

    par_t[:, 0:ROWS] = merged([leaf_t[pl.ds(c, 64, stride=8), :] for c in range(8)])
    gra_t[:, 0:ROWS] = merged([par_t[pl.ds(c, 8, stride=8), :] for c in range(8)])
    msg[...] = jnp.zeros_like(msg)
    msg[:, 0:ROWS] = merged([jnp.broadcast_to(gra_t[c : c + 1, :], (8, 128)) for c in range(8)])

    def send_top(i, c):
        to = lax.rem(g + i, grps)
        copy(msg, buf_a.at[g], send_a.at[i], recv_a.at[g], (to, d)).start()
        return c

    lax.fori_loop(1, grps, send_top, 0)

    both = jnp.concatenate([par_t[...], gra_t[...], jnp.zeros((56, 128), F32)], axis=0)
    midm[...] = both.T[0:112].astype(BF)
    mid_up = copy(midm, midg.at[0], send_m.at[0], recv_m.at[0], at(above))
    mid_dn = copy(midm, midg.at[1], send_m.at[1], recv_m.at[1], at(below))
    mid_up.start()
    mid_dn.start()

    nclass = leaf_lists.shape[0]
    for r in lists_in[1:]:
        r.wait()
    ml_ref[0:64, 0:nclass] = par_l[...]
    ml_ref[64:72, 0:nclass] = gra_l[...]
    mt_ref[0:128, :] = ml_ref[:, 0:128].T
    mt_ref[128:256, :] = ml_ref[:, 128:256].T
    for q in range(98):
        s_ref[pl.ds(q, 8, stride=ROWS), 0:98] = sp[q].astype(F32)
    sub8 = lax.broadcasted_iota(jnp.int32, (8, 128), 0)

    def wait_top(i, c):
        frm = lax.rem(g + i, grps)
        w = copy(msg, buf_a.at[frm], send_a.at[i], recv_a.at[frm], (frm, d))
        w.wait_send()
        w.wait_recv()
        return jnp.where(sub8 == frm, buf_a[frm], c)

    def send_x(i, c):
        copy(msg_b, buf_b.at[x], send_b.at[i], recv_b.at[x], (g, lax.rem(d + ZS * i, devs))).start()
        return c

    def pass_x():
        msg_b[...] = lax.fori_loop(1, grps, wait_top, msg[...])
        lax.fori_loop(1, xs, send_x, 0)

    def wait_x(i, c):
        to = lax.rem(d + ZS * i, devs)
        frm = to // ZS
        w = copy(msg_b, buf_b.at[frm], send_b.at[i], recv_b.at[frm], (g, to))
        w.wait_send()
        w.wait_recv()
        ring[0, 0, frm] = buf_b[frm]
        ring[1, 0, frm] = buf_b[frm]
        return c

    def hops(k):
        return (
            copy(ring.at[0, k], ring.at[0, k + 1], send_z.at[0, k], recv_z.at[0, k + 1], z_up),
            copy(ring.at[1, k], ring.at[1, k + 1], send_z.at[1, k], recv_z.at[1, k + 1], z_down),
        )

    def hop_first():
        ring[0, 0, x] = msg_b[...]
        ring[1, 0, x] = msg_b[...]
        lax.fori_loop(1, xs, wait_x, 0)
        for c in hops(0):
            c.start()

    def hop_next(k):
        for c in hops(k - 1):
            c.wait()
        for c in hops(k):
            c.start()

    def mid_class(row, base):
        e = jnp.broadcast_to(row, (16, 128))
        lo = (e & 127).astype(jnp.int16)
        is_p = ((lane < 64) & (e >= 0)).astype(jnp.int16) > 0
        is_g = ((lane >= 64) & (lane < 72) & (e >= 0)).astype(jnp.int16) > 0
        for v in range(7):
            rows = slice(16 * v, 16 * v + 16)
            x = jnp.zeros((16, 128), BF)
            x = jnp.where(is_p, take_lanes(pwin[rows, :], lo), x)
            x = jnp.where(is_g, take_lanes(gwin[rows, :], lo), x)
            g_ref[base + 16 * v : base + 16 * v + 16, 512:640] = x

    def group(k0, n, early=None):
        rows = lists_of(k0, n)
        mids = [mt_ref[pl.ds(k0 + i, min(8, n - i)), :] for i in range(0, n, 8)]
        for q in range(98):
            a_ref[pl.ds(q, n, stride=ROWS), 0:98] = tr[q, pl.ds(k0, n), :].astype(F32)
        for c in range(n):
            new = g_ref.at[pl.ds(c * 128, 128), :]
            if early is None:
                pick(c, rows[c], None, new, (1, 2, 0, 3))
            else:
                pick(c, rows[c], go_ref.at[early, pl.ds(c * 128, 128), :], new, (0, 3))
            mid_class(mids[c // 8][c % 8 : c % 8 + 1], c * 128)
        for i in range(0, n, 8):
            m = min(8, n - i)
            ops = jnp.concatenate(
                [a_ref[(i + c) * ROWS : (i + c + 1) * ROWS, :].astype(BF) for c in range(m)], axis=1
            )
            acc_ref[...] += jnp.dot(
                ops, g_ref[i * 128 : (i + m) * 128, :], preferred_element_type=F32
            )

    lax.fori_loop(ahead, EARLY, lambda j, c: (own_group(j), c)[1], 0)
    leaf_up.wait()
    leaf_dn.wait()
    place(2, (0, 3), (got.at[0], got.at[1]))
    mid_up.wait()
    mid_dn.wait()
    at = lax.broadcasted_iota(jnp.int16, (16, 128), 1)
    for v in range(7):
        rows = slice(16 * v, 16 * v + 16)
        low, own, high = midg[0, rows, :], midm[rows, :], midg[1, rows, :]
        pwin[rows, :] = jnp.where(
            at < 32,
            take_lanes(low, (at + jnp.int16(32)) & jnp.int16(127)),
            jnp.where(
                at < 96,
                take_lanes(own, (at - jnp.int16(32)) & jnp.int16(127)),
                take_lanes(high, (at - jnp.int16(96)) & jnp.int16(127)),
            ),
        )
        gwin[rows, :] = jnp.where(
            at < 4,
            take_lanes(low, (at + jnp.int16(68)) & jnp.int16(127)),
            jnp.where(
                at < 12,
                take_lanes(own, (at + jnp.int16(60)) & jnp.int16(127)),
                take_lanes(high, (at + jnp.int16(52)) & jnp.int16(127)),
            ),
        )
    tr_in.wait()

    def late_step(j, carry):
        @pl.when(j == 0)
        def _():
            pass_x()

        @pl.when(j == 2)
        def _():
            hop_first()

        @pl.when((lax.rem(j, 2) == 0) & (j >= 4) & (j < ZS + 2))
        def _():
            hop_next((j - 2) // 2)

        group(pl.multiple_of(j * 16, 16), 16, j)
        return carry

    def step(j, carry):
        @pl.when((lax.rem(j, 2) == 0) & (j < ZS + 2))
        def _():
            hop_next((j - 2) // 2)

        group(pl.multiple_of(j * 16, 16), 16)
        return carry

    full = nclass // 16
    lax.fori_loop(0, EARLY, late_step, 0)
    lax.fori_loop(EARLY, full, step, 0)
    for c in hops(ZS // 2 - 1):
        c.wait()
    for k in range(ZS // 2 + 1):
        tops[lax.rem(z + ZS - k, ZS)] = ring[0, k]
    for k in range(1, ZS // 2):
        tops[lax.rem(z + k, ZS)] = ring[1, k]
    t = top_l[...]
    t = jnp.broadcast_to(jnp.where(t >= 0, (t & 7) * 32 + (t & 24) + (t >> 5), -1), (256, nclass))
    named_at = jnp.where(lax.broadcasted_iota(jnp.int32, (256, nclass), 0) == t, 1.0, 0.0).astype(BF)
    table = tops[...].reshape(256, 128).astype(BF)
    named = lax.dot_general(named_at, table, (((0,), (0,)), ((), ())), preferred_element_type=F32)[:, 0:98]

    def top_rows(first, last):
        for q in range(first, last):
            tsum_ref[q : q + 1, 0:98] = jnp.sum(tr[q].astype(F32) * named, axis=0, keepdims=True)

    spread = s_ref[...].astype(BF)
    lanes = lax.broadcasted_iota(jnp.int32, (ROWS, 128), 1)

    def spread_from(v, index):
        kids = (v if index is None else take_lanes(v, index)).astype(BF)
        y = jnp.dot(
            spread,
            jnp.concatenate([kids, jnp.zeros((128 - ROWS, 128), BF)], axis=0),
            preferred_element_type=F32,
        )
        r = y[0:ROWS]
        for c in range(1, 8):
            r = jnp.where((lanes & 7) == c, y[c * ROWS : (c + 1) * ROWS], r)
        return r

    k0 = full * 16
    n = nclass - k0
    rows = lists_of(k0, n)
    mids = [mt_ref[k0 + i : k0 + min(i + 8, n), :] for i in range(0, n, 8)]
    for q in range(98):
        a_ref[pl.ds(q, n, stride=ROWS), 0:98] = tr[q, k0:nclass, :].astype(F32)
    ops = jnp.concatenate([a_ref[c * ROWS : (c + 1) * ROWS, :].astype(BF) for c in range(n)], axis=1)
    for c in range(n):
        mid_class(mids[c // 8][c % 8 : c % 8 + 1], c * 128)
    mid = acc_ref[:, 512:640] + jnp.dot(ops, g_ref[0 : n * 128, 512:640], preferred_element_type=F32)
    for c in range(n):
        pick(c, rows[c], None, g_ref.at[c * 128 : (c + 1) * 128, :], (1, 2, 0, 3))
        if c < 7:
            top_rows(14 * c, 14 * c + 14)
        if c == 7:
            top = jnp.broadcast_to(0.125 * jnp.sum(tsum_ref[...], axis=1, keepdims=True), (ROWS, 128))
            grand = 0.25 * mid + spread_from(top, None)
        if c == 9:
            parent = 0.5 * mid + spread_from(grand, 64 + ((lanes >> 3) & 7))
    leaf = acc_ref[:, 0:512] + jnp.dot(ops, g_ref[0 : n * 128, 0:512], preferred_element_type=F32)
    for i in range(4):
        cols = slice(128 * i, 128 * i + 128)
        out[:, cols] = (leaf[:, cols] + spread_from(parent, 16 * i + (lanes >> 3)))[0:98]


def solution(mesh):
    grps, devs = mesh.shape["grp"], mesh.shape["dev"]

    def per_device(
        strengths, source_counts, source_map, merge_ops, translate_ops, spread_ops,
        leaf_lists, parent_lists, grand_lists, top_lists,
    ):
        args = (
            strengths, source_counts.reshape(1, -1), source_map.T, merge_ops.transpose(1, 0, 2),
            leaf_lists, parent_lists.T, grand_lists.T, top_lists.T,
            translate_ops.transpose(1, 0, 2), spread_ops.transpose(1, 0, 2),
        )
        dma = pltpu.SemaphoreType.DMA
        vm = pltpu.VMEM
        return pl.pallas_call(
            lambda *refs: kernel(grps, devs, *refs),
            out_shape=jax.ShapeDtypeStruct((98, leaf_lists.shape[1]), F32),
            in_specs=[pl.BlockSpec(memory_space=pl.ANY)] * len(args),
            out_specs=pl.BlockSpec(memory_space=pltpu.VMEM),
            scratch_shapes=[vm(a.shape, a.dtype) for a in args]
            + [
                vm((8 * ROWS, 128), F32),
                vm((512, 128), F32),
                vm((64, 128), F32),
                vm((8, 128), F32),
                vm((2, 112, 256), BF),
                vm((2, 112, 256), BF),
                vm((112, 128), BF),
                vm((2, 112, 128), BF),
                vm((8, 128), F32),
                vm((grps, 8, 128), F32),
                vm((8, 128), F32),
                vm((devs // ZS, 8, 128), F32),
                vm((2, ZS // 2 + 1, devs // ZS, 8, 128), F32),
                vm((ZS, devs // ZS, grps, 128), F32),
                vm((4 * ROWS, 256), BF),
                vm((112, 1024), BF),
                vm((112, 128), BF),
                vm((112, 128), BF),
                vm((EARLY, 16 * 128, 512), BF),
                vm((16 * 128, 640), BF),
                vm((16 * ROWS, 128), F32),
                vm((8 * ROWS, 128), F32),
                vm((128, 256), jnp.int32),
                vm((256, 128), jnp.int32),
                vm((ROWS, 640), F32),
                vm((ROWS, 128), F32),
                dma((10,)),
                dma((2,)), dma((2,)), dma((2,)), dma((2,)),
                dma((grps,)), dma((grps,)), dma((devs // ZS,)), dma((devs // ZS,)),
                dma((2, ZS // 2 + 1)), dma((2, ZS // 2 + 1)),
            ],
            compiler_params=pltpu.CompilerParams(
                collective_id=0, has_side_effects=True, vmem_limit_bytes=48 << 20
            ),
            name="fmm",
        )(*[pltpu.with_memory_space_constraint(a, pltpu.HBM) for a in args])

    rows = P(("grp", "dev"))
    cols = P(None, ("grp", "dev"))
    return jax.shard_map(
        per_device,
        mesh=mesh,
        in_specs=(P(("grp", "dev"), None), rows, P(), P(), P(), P(), cols, cols, cols, cols),
        out_specs=cols,
        check_vma=False,
    )
```

```python
import jax
import jax.numpy as jnp
from jax import lax
from jax.experimental import pallas as pl
from jax.experimental.pallas import tpu as pltpu
from jax.sharding import PartitionSpec as P

BF = jnp.bfloat16
F32 = jnp.float32
ROWS = 104
DEEP = 112
MESH = pl.DeviceIdType.MESH
ZS = 8
LANES = (2, 6, 10, 14)
EARLY = 7
NT = (((1,), (1,)), ((), ()))


def take_lanes(x, index):
    dims = lax.GatherDimensionNumbers(
        offset_dims=(),
        collapsed_slice_dims=(1,),
        start_index_map=(1,),
        operand_batching_dims=(0,),
        start_indices_batching_dims=(0,),
    )
    return lax.gather(
        x, index[..., None], dims, slice_sizes=(1, 1), mode=lax.GatherScatterMode.PROMISE_IN_BOUNDS
    )


def kernel(
    grps, devs,
    strengths_h, counts_h, smap_h, mg_h, leaf_lists_h, par_h, gra_h, top_h, tr_h, sp_h, out,
    strengths, counts, smap, mg, leaf_lists, par_l, gra_l, top_l, tr, sp,
    m_ref, leaf_t, par_t, gra_t, mine, got, midm, midg, msg, buf_a, msg_b, buf_b, ring, tops,
    w4, win, pwin, gwin, go_ref, g_ref, a_ref, s_ref, ml_ref, mt_ref, acc_ref, tsum_ref,
    load_sem, send_l, recv_l, send_m, recv_m, send_a, recv_a, send_b, recv_b, send_z, recv_z,
):
    g = lax.axis_index("grp")
    d = lax.axis_index("dev")
    total = grps * devs
    xs = devs // ZS
    x = d // ZS
    me = g * devs + d
    above = lax.rem(me + 1, total)
    below = lax.rem(me + total - 1, total)

    def at(pos):
        return (pos // devs, lax.rem(pos, devs))

    def load(src, dst, k):
        c = pltpu.make_async_copy(src, dst, load_sem.at[k])
        c.start()
        return c

    strengths_in = load(strengths_h, strengths, 0)
    counts_in = load(counts_h, counts, 1)
    smap_in = load(smap_h, smap, 2)
    mg_in = load(mg_h, mg, 3)
    lists_in = [
        load(h, v, 4 + i)
        for i, (h, v) in enumerate(
            ((leaf_lists_h, leaf_lists), (par_h, par_l), (gra_h, gra_l), (top_h, top_l), (sp_h, sp))
        )
    ]
    tr_in = load(tr_h, tr, 9)
    barrier = pltpu.get_barrier_semaphore()

    def greet(pos):
        pl.semaphore_signal(barrier, inc=1, device_id=pos, device_id_type=MESH)

    z = lax.rem(d, ZS)
    first = d - z
    z_up = (g, first + lax.rem(z + 1, ZS))
    z_down = (g, first + lax.rem(z + ZS - 1, ZS))
    greet(at(above))
    greet(at(below))
    greet(z_up)
    greet(z_down)
    lax.fori_loop(1, grps, lambda i, c: (greet((lax.rem(g + i, grps), d)), c)[1], 0)
    lax.fori_loop(1, xs, lambda i, c: (greet((g, lax.rem(d + ZS * i, devs))), c)[1], 0)

    for r in (leaf_t, par_t, gra_t, m_ref, a_ref, s_ref, acc_ref, tsum_ref):
        r[...] = jnp.zeros_like(r)
    g_ref[...] = jnp.zeros_like(g_ref)
    ml_ref[...] = jnp.full_like(ml_ref, -1)
    for r in (strengths_in, counts_in, smap_in):
        r.wait()
    cnt = jnp.concatenate(
        [jnp.broadcast_to(counts[:, 128 * i : 128 * i + 128], (128, 128)).T for i in range(4)], axis=0
    ).astype(jnp.int16)
    slot = lax.broadcasted_iota(jnp.int16, (512, 128), 1)
    zero = jnp.zeros((512, 128), BF)
    live = jnp.concatenate(
        [
            jnp.where(slot < cnt, strengths[:, 0:128], zero),
            jnp.where(slot + jnp.int16(128) < cnt, strengths[:, 128:256], zero),
        ],
        axis=1,
    )
    lt = lax.dot_general(live, smap[...], NT, preferred_element_type=F32)
    leaf_t[:, 0:98] = lt.astype(BF).astype(F32)
    for half in range(2):
        mine[half] = jnp.concatenate(
            [leaf_t[256 * half + 128 * i : 256 * half + 128 * i + 128, :].T[0:112] for i in range(2)], axis=1
        ).astype(BF)

    def copy(src, dst, ss, rs, pos):
        return pltpu.make_async_remote_copy(
            src_ref=src, dst_ref=dst, send_sem=ss, recv_sem=rs, device_id=pos, device_id_type=MESH
        )

    sub = lax.broadcasted_iota(jnp.int16, (16, 512), 0)
    lane = lax.broadcasted_iota(jnp.int32, (16, 128), 1)

    def place(slot, blocks, parts):
        w4[slot * ROWS : (slot + 2) * ROWS, :] = jnp.concatenate(
            [p[...].astype(F32)[0:ROWS] for p in parts], axis=0
        ).astype(BF)
        for h, p in zip(blocks, parts):
            win[:, 256 * h : 256 * h + 256] = p[...]

    def leaf_class(row, old, new, blocks):
        lo = jnp.broadcast_to(row & 255, (16, 512)).astype(jnp.int16)
        hi = row >> 8
        onehot = jnp.concatenate(
            [jnp.where(lo - jnp.int16(16 * i) == sub, BF(1), BF(0)) for i in range(16)], axis=0
        )
        at0 = 2 * ROWS if blocks[0] == 0 else 0
        r = jnp.dot(w4[at0 : at0 + len(blocks) * ROWS, :], onehot, preferred_element_type=F32)
        picked = jnp.zeros((ROWS, 512), F32) if old is None else old[0:ROWS, :].astype(F32)
        for i, h in enumerate(blocks):
            hit = jnp.broadcast_to(hi == h, (ROWS, 512))
            picked = jnp.where(hit, r[i * ROWS : (i + 1) * ROWS], picked)
        new[0:ROWS, 0:512] = picked.astype(BF)

    def lanes_class(row, old, new, blocks):
        for i in range(4):
            cols = slice(128 * i, 128 * i + 128)
            e = jnp.broadcast_to(row[:, cols], (16, 128))
            lo = (e & 127).astype(jnp.int16)
            hi = (e >> 7).astype(jnp.int16)
            sources = [b for h in blocks for b in (2 * h, 2 * h + 1)]
            hits = [hi == jnp.int16(b) for b in sources]
            for v in range(7):
                rows = slice(16 * v, 16 * v + 16)
                p = jnp.zeros((16, 128), BF) if old is None else old[rows, cols]
                for hit, b in zip(hits, sources):
                    p = jnp.where(hit, take_lanes(win[rows, 128 * b : 128 * b + 128], lo), p)
                new[rows, cols] = p

    def lists_of(k0, n):
        lists = [leaf_lists[pl.ds(k0 + i, min(8, n - i)), :] for i in range(0, n, 8)]
        return [lists[c // 8][c % 8 : c % 8 + 1] for c in range(n)]

    def pick(c, *rest):
        (lanes_class if c in LANES else leaf_class)(*rest)

    def own_group(j):
        rows = lists_of(pl.multiple_of(j * 16, 16), 16)
        for c in range(16):
            pick(c, rows[c], None, go_ref.at[j, pl.ds(c * 128, 128), :], (1, 2))

    place(0, (1, 2), (mine.at[0], mine.at[1]))
    lists_in[0].wait()
    ahead = jnp.where(z == 0, 4, jnp.where(z == 1, 2, 0))
    lax.fori_loop(0, ahead, lambda j, c: (own_group(j), c)[1], 0)
    pl.semaphore_wait(barrier, 4 + grps - 1 + xs - 1)
    leaf_up = copy(mine.at[1], got.at[0], send_l.at[0], recv_l.at[0], at(above))
    leaf_dn = copy(mine.at[0], got.at[1], send_l.at[1], recv_l.at[1], at(below))
    leaf_up.start()
    leaf_dn.start()

    mg_in.wait()
    for q in range(98):
        m_ref[pl.ds(q, 8, stride=ROWS), 0:98] = mg[q].astype(F32)
    merge = jnp.concatenate([m_ref[ROWS * c : ROWS * c + ROWS, :].astype(BF) for c in range(8)], axis=1)

    def merged(kids):
        x = jnp.concatenate([k.astype(BF) for k in kids], axis=1)
        y = lax.dot_general(x, merge, NT, preferred_element_type=F32)
        return y.astype(BF).astype(F32)

    par_t[:, 0:ROWS] = merged([leaf_t[pl.ds(c, 64, stride=8), :] for c in range(8)])
    gra_t[:, 0:ROWS] = merged([par_t[pl.ds(c, 8, stride=8), :] for c in range(8)])
    msg[...] = jnp.zeros_like(msg)
    msg[:, 0:ROWS] = merged([jnp.broadcast_to(gra_t[c : c + 1, :], (8, 128)) for c in range(8)])

    def send_top(i, c):
        to = lax.rem(g + i, grps)
        copy(msg, buf_a.at[g], send_a.at[i], recv_a.at[g], (to, d)).start()
        return c

    lax.fori_loop(1, grps, send_top, 0)

    both = jnp.concatenate([par_t[...], gra_t[...], jnp.zeros((56, 128), F32)], axis=0)
    midm[...] = both.T[0:112].astype(BF)
    mid_up = copy(midm, midg.at[0], send_m.at[0], recv_m.at[0], at(above))
    mid_dn = copy(midm, midg.at[1], send_m.at[1], recv_m.at[1], at(below))
    mid_up.start()
    mid_dn.start()

    nclass = leaf_lists.shape[0]
    for r in lists_in[1:]:
        r.wait()
    ml_ref[0:64, 0:nclass] = par_l[...]
    ml_ref[64:72, 0:nclass] = gra_l[...]
    mt_ref[0:128, :] = ml_ref[:, 0:128].T
    mt_ref[128:256, :] = ml_ref[:, 128:256].T
    for q in range(98):
        s_ref[pl.ds(q, 8, stride=ROWS), 0:98] = sp[q].astype(F32)
    sub8 = lax.broadcasted_iota(jnp.int32, (8, 128), 0)

    def wait_top(i, c):
        frm = lax.rem(g + i, grps)
        w = copy(msg, buf_a.at[frm], send_a.at[i], recv_a.at[frm], (frm, d))
        w.wait_send()
        w.wait_recv()
        return jnp.where(sub8 == frm, buf_a[frm], c)

    def send_x(i, c):
        copy(msg_b, buf_b.at[x], send_b.at[i], recv_b.at[x], (g, lax.rem(d + ZS * i, devs))).start()
        return c

    def pass_x():
        msg_b[...] = lax.fori_loop(1, grps, wait_top, msg[...])
        lax.fori_loop(1, xs, send_x, 0)

    def wait_x(i, c):
        to = lax.rem(d + ZS * i, devs)
        frm = to // ZS
        w = copy(msg_b, buf_b.at[frm], send_b.at[i], recv_b.at[frm], (g, to))
        w.wait_send()
        w.wait_recv()
        ring[0, 0, frm] = buf_b[frm]
        ring[1, 0, frm] = buf_b[frm]
        return c

    def hops(k):
        return (
            copy(ring.at[0, k], ring.at[0, k + 1], send_z.at[0, k], recv_z.at[0, k + 1], z_up),
            copy(ring.at[1, k], ring.at[1, k + 1], send_z.at[1, k], recv_z.at[1, k + 1], z_down),
        )

    def hop_first():
        ring[0, 0, x] = msg_b[...]
        ring[1, 0, x] = msg_b[...]
        lax.fori_loop(1, xs, wait_x, 0)
        for c in hops(0):
            c.start()

    def hop_next(k):
        for c in hops(k - 1):
            c.wait()
        for c in hops(k):
            c.start()

    def mid_class(row, base):
        e = jnp.broadcast_to(row, (16, 128))
        lo = (e & 127).astype(jnp.int16)
        is_p = ((lane < 64) & (e >= 0)).astype(jnp.int16) > 0
        is_g = ((lane >= 64) & (lane < 72) & (e >= 0)).astype(jnp.int16) > 0
        for v in range(7):
            rows = slice(16 * v, 16 * v + 16)
            x = jnp.zeros((16, 128), BF)
            x = jnp.where(is_p, take_lanes(pwin[rows, :], lo), x)
            x = jnp.where(is_g, take_lanes(gwin[rows, :], lo), x)
            g_ref[base + 16 * v : base + 16 * v + 16, 512:640] = x

    def group(k0, n, early=None):
        rows = lists_of(k0, n)
        mids = [mt_ref[pl.ds(k0 + i, min(8, n - i)), :] for i in range(0, n, 8)]
        for q in range(98):
            a_ref[pl.ds(q, n, stride=ROWS), 0:98] = tr[q, pl.ds(k0, n), :].astype(F32)
        for c in range(n):
            new = g_ref.at[pl.ds(c * DEEP, DEEP), :]
            if early is None:
                pick(c, rows[c], None, new, (1, 2, 0, 3))
            else:
                pick(c, rows[c], go_ref.at[early, pl.ds(c * 128, 128), :], new, (0, 3))
            mid_class(mids[c // 8][c % 8 : c % 8 + 1], c * DEEP)
        ops = jnp.concatenate(
            [a_ref[c * ROWS : (c + 1) * ROWS, 0:DEEP].astype(BF) for c in range(n)], axis=1
        )
        acc_ref[...] += jnp.dot(ops, g_ref[0 : n * DEEP, :], preferred_element_type=F32)

    lax.fori_loop(ahead, EARLY, lambda j, c: (own_group(j), c)[1], 0)
    leaf_up.wait()
    leaf_dn.wait()
    place(2, (0, 3), (got.at[0], got.at[1]))
    mid_up.wait()
    mid_dn.wait()
    at = lax.broadcasted_iota(jnp.int16, (16, 128), 1)
    for v in range(7):
        rows = slice(16 * v, 16 * v + 16)
        low, own, high = midg[0, rows, :], midm[rows, :], midg[1, rows, :]
        pwin[rows, :] = jnp.where(
            at < 32,
            take_lanes(low, (at + jnp.int16(32)) & jnp.int16(127)),
            jnp.where(
                at < 96,
                take_lanes(own, (at - jnp.int16(32)) & jnp.int16(127)),
                take_lanes(high, (at - jnp.int16(96)) & jnp.int16(127)),
            ),
        )
        gwin[rows, :] = jnp.where(
            at < 4,
            take_lanes(low, (at + jnp.int16(68)) & jnp.int16(127)),
            jnp.where(
                at < 12,
                take_lanes(own, (at + jnp.int16(60)) & jnp.int16(127)),
                take_lanes(high, (at + jnp.int16(52)) & jnp.int16(127)),
            ),
        )
    tr_in.wait()

    def late_step(j, carry):
        @pl.when(j == 0)
        def _():
            pass_x()

        @pl.when(j == 2)
        def _():
            hop_first()

        @pl.when((lax.rem(j, 2) == 0) & (j >= 4) & (j < ZS + 2))
        def _():
            hop_next((j - 2) // 2)

        group(pl.multiple_of(j * 16, 16), 16, j)
        return carry

    def step(j, carry):
        @pl.when((lax.rem(j, 2) == 0) & (j < ZS + 2))
        def _():
            hop_next((j - 2) // 2)

        group(pl.multiple_of(j * 16, 16), 16)
        return carry

    full = nclass // 16
    lax.fori_loop(0, EARLY, late_step, 0)
    lax.fori_loop(EARLY, full, step, 0)
    for c in hops(ZS // 2 - 1):
        c.wait()
    for k in range(ZS // 2 + 1):
        tops[lax.rem(z + ZS - k, ZS)] = ring[0, k]
    for k in range(1, ZS // 2):
        tops[lax.rem(z + k, ZS)] = ring[1, k]
    t = top_l[...]
    t = jnp.broadcast_to(jnp.where(t >= 0, (t & 7) * 32 + (t & 24) + (t >> 5), -1), (256, nclass))
    named_at = jnp.where(lax.broadcasted_iota(jnp.int32, (256, nclass), 0) == t, 1.0, 0.0).astype(BF)
    table = tops[...].reshape(256, 128).astype(BF)
    named = lax.dot_general(named_at, table, (((0,), (0,)), ((), ())), preferred_element_type=F32)[:, 0:98]

    def top_rows(first, last):
        for q in range(first, last):
            tsum_ref[q : q + 1, 0:98] = jnp.sum(tr[q].astype(F32) * named, axis=0, keepdims=True)

    spread = s_ref[...].astype(BF)
    lanes = lax.broadcasted_iota(jnp.int32, (ROWS, 128), 1)

    def spread_from(v, index):
        kids = (v if index is None else take_lanes(v, index)).astype(BF)
        y = jnp.dot(
            spread,
            jnp.concatenate([kids, jnp.zeros((128 - ROWS, 128), BF)], axis=0),
            preferred_element_type=F32,
        )
        r = y[0:ROWS]
        for c in range(1, 8):
            r = jnp.where((lanes & 7) == c, y[c * ROWS : (c + 1) * ROWS], r)
        return r

    k0 = full * 16
    n = nclass - k0
    rows = lists_of(k0, n)
    mids = [mt_ref[k0 + i : k0 + min(i + 8, n), :] for i in range(0, n, 8)]
    for q in range(98):
        a_ref[pl.ds(q, n, stride=ROWS), 0:98] = tr[q, k0:nclass, :].astype(F32)
    ops = jnp.concatenate([a_ref[c * ROWS : (c + 1) * ROWS, 0:DEEP].astype(BF) for c in range(n)], axis=1)
    for c in range(n):
        mid_class(mids[c // 8][c % 8 : c % 8 + 1], c * DEEP)
    mid = acc_ref[:, 512:640] + jnp.dot(ops, g_ref[0 : n * DEEP, 512:640], preferred_element_type=F32)
    for c in range(n):
        pick(c, rows[c], None, g_ref.at[c * DEEP : (c + 1) * DEEP, :], (1, 2, 0, 3))
        if c < 7:
            top_rows(14 * c, 14 * c + 14)
        if c == 7:
            top = jnp.broadcast_to(0.125 * jnp.sum(tsum_ref[...], axis=1, keepdims=True), (ROWS, 128))
            grand = 0.25 * mid + spread_from(top, None)
        if c == 9:
            parent = 0.5 * mid + spread_from(grand, 64 + ((lanes >> 3) & 7))
    leaf = acc_ref[:, 0:512] + jnp.dot(ops, g_ref[0 : n * DEEP, 0:512], preferred_element_type=F32)
    for i in range(4):
        cols = slice(128 * i, 128 * i + 128)
        out[:, cols] = (leaf[:, cols] + spread_from(parent, 16 * i + (lanes >> 3)))[0:98]


def solution(mesh):
    grps, devs = mesh.shape["grp"], mesh.shape["dev"]

    def per_device(
        strengths, source_counts, source_map, merge_ops, translate_ops, spread_ops,
        leaf_lists, parent_lists, grand_lists, top_lists,
    ):
        args = (
            strengths, source_counts.reshape(1, -1), source_map.T, merge_ops.transpose(1, 0, 2),
            leaf_lists, parent_lists.T, grand_lists.T, top_lists.T,
            translate_ops.transpose(1, 0, 2), spread_ops.transpose(1, 0, 2),
        )
        dma = pltpu.SemaphoreType.DMA
        vm = pltpu.VMEM
        return pl.pallas_call(
            lambda *refs: kernel(grps, devs, *refs),
            out_shape=jax.ShapeDtypeStruct((98, leaf_lists.shape[1]), F32),
            in_specs=[pl.BlockSpec(memory_space=pl.ANY)] * len(args),
            out_specs=pl.BlockSpec(memory_space=pltpu.VMEM),
            scratch_shapes=[vm(a.shape, a.dtype) for a in args]
            + [
                vm((8 * ROWS, 128), F32),
                vm((512, 128), F32),
                vm((64, 128), F32),
                vm((8, 128), F32),
                vm((2, 112, 256), BF),
                vm((2, 112, 256), BF),
                vm((112, 128), BF),
                vm((2, 112, 128), BF),
                vm((8, 128), F32),
                vm((grps, 8, 128), F32),
                vm((8, 128), F32),
                vm((devs // ZS, 8, 128), F32),
                vm((2, ZS // 2 + 1, devs // ZS, 8, 128), F32),
                vm((ZS, devs // ZS, grps, 128), F32),
                vm((4 * ROWS, 256), BF),
                vm((112, 1024), BF),
                vm((112, 128), BF),
                vm((112, 128), BF),
                vm((EARLY, 16 * 128, 512), BF),
                vm((16 * 128, 640), BF),
                vm((16 * ROWS, 128), F32),
                vm((8 * ROWS, 128), F32),
                vm((128, 256), jnp.int32),
                vm((256, 128), jnp.int32),
                vm((ROWS, 640), F32),
                vm((ROWS, 128), F32),
                dma((10,)),
                dma((2,)), dma((2,)), dma((2,)), dma((2,)),
                dma((grps,)), dma((grps,)), dma((devs // ZS,)), dma((devs // ZS,)),
                dma((2, ZS // 2 + 1)), dma((2, ZS // 2 + 1)),
            ],
            compiler_params=pltpu.CompilerParams(
                collective_id=0, has_side_effects=True, vmem_limit_bytes=48 << 20
            ),
            name="fmm",
        )(*[pltpu.with_memory_space_constraint(a, pltpu.HBM) for a in args])

    rows = P(("grp", "dev"))
    cols = P(None, ("grp", "dev"))
    return jax.shard_map(
        per_device,
        mesh=mesh,
        in_specs=(P(("grp", "dev"), None), rows, P(), P(), P(), P(), cols, cols, cols, cols),
        out_specs=cols,
        check_vma=False,
    )
```
